128 devices in a mesh: px: 16 (over x_lo, y, core), py: 8 (over z, x_hi).
Axes of the slice: x: 4 (x_hi: 2, x_lo: 2; x = x_hi * 2 + x_lo), y: 4, z: 4, core: 2. Of those that a mesh axis runs over, the one named last changes fastest.
Arguments:
- field: float32 [1, 48, 128, 128, 256], P(None, None, 'px', 'py'), may hold values from -6 to 6
- spectral_weight: float32 [2, 32, 32, 32, 2304], P(None, 'py', None, 'px'), may hold values from -6 to 6
- pointwise_weight: float32 [48, 48], replicated, may hold values from -0.875 to 0.875
- channel_bias: float32 [48], replicated, may hold values from -3 to 3
Outputs:
- layer_out: float32 [1, 48, 128, 128, 256], P(None, None, 'px', 'py')
The draws below stay inside these ranges and needn't reach their ends.
All inputs are finite; a program needn't handle non-finite values.
Results may differ from the reference program's by a relative error of at most 0.000065.
Values sent between devices are 32-bit elements; how exact they have to be, the bound alone decides.
A program may use at most 128 MiB of HBM per device.

```python
import math
import jax
import jax.numpy as jnp
from jax import lax

BATCH = 1
CH = 48
NX = 128
NY = 128
NZ = 256
MODES = 32


def level_of(stream_key, dims, cuts, smallest, top_value):
    def one(dim, blocks):
        heights = jax.random.uniform(jax.random.fold_in(jax.random.fold_in(stream_key, 6), dim), (blocks,), jnp.float32, smallest / len(cuts), top_value / len(cuts))
        return jnp.repeat(jnp.exp(heights), dims[dim] // blocks).reshape((-1,) + (1,) * (len(dims) - dim - 1))

    gain = one(*cuts[0])
    for cut in cuts[1:]:
        gain = gain * one(*cut)
    return gain


def normal_values(rng, dims, deviation, reach, pieces=(), held_as=jnp.bfloat16):
    values = deviation * jax.random.normal(rng, dims, jnp.float32)
    if pieces:
        values = values * level_of(rng, dims, pieces, -0.22, 0.18)
    return jnp.clip(values, -reach, reach).astype(held_as)


def setup_inputs(seed: int = 0) -> dict:
    key_of = jax.random.split(jax.random.key(seed), 5)
    return {
        "field": normal_values(key_of[0], (BATCH, CH, NX, NY, NZ), 1.0, 6.0, ((2, 16), (3, 8)), jnp.float32),
        "spectral_weight": normal_values(key_of[1], (2, MODES, MODES, MODES, CH * CH), 1.0, 6.0, ((1, 8), (3, 16)), jnp.float32),
        "pointwise_weight": normal_values(key_of[2], (CH, CH), CH ** -0.5, 0.875, (), jnp.float32),
        "channel_bias": normal_values(key_of[3], (CH,), 0.5, 3.0, (), jnp.float32),
    }


def tables(modes, length, signed):
    index = jnp.arange(length, dtype=jnp.int32)
    number = jnp.arange(modes, dtype=jnp.int32)
    if signed:
        number = jnp.where(number < modes // 2, number, number - modes)
    product = jnp.mod(index[:, None] * number[None, :], length)
    angle = product.astype(jnp.float32) * (2.0 * math.pi / length)
    return jnp.cos(angle), jnp.sin(angle)


def reference(field, spectral_weight, pointwise_weight, channel_bias):
    precise = lax.Precision.HIGHEST
    z_cos, z_sin = tables(MODES, NZ, False)
    x_cos, x_sin = tables(MODES, NX, True)
    y_cos, y_sin = tables(MODES, NY, True)
    z_real = jnp.einsum("bcxyz,zk->bxykc", field, z_cos, precision=precise)
    z_imag = -jnp.einsum("bcxyz,zk->bxykc", field, z_sin, precision=precise)
    x_real = jnp.einsum("bxykc,xi->biykc", z_real, x_cos, precision=precise) + jnp.einsum("bxykc,xi->biykc", z_imag, x_sin, precision=precise)
    x_imag = jnp.einsum("bxykc,xi->biykc", z_imag, x_cos, precision=precise) - jnp.einsum("bxykc,xi->biykc", z_real, x_sin, precision=precise)
    y_real = jnp.einsum("biykc,yj->bijkc", x_real, y_cos, precision=precise) + jnp.einsum("biykc,yj->bijkc", x_imag, y_sin, precision=precise)
    y_imag = jnp.einsum("biykc,yj->bijkc", x_imag, y_cos, precision=precise) - jnp.einsum("biykc,yj->bijkc", x_real, y_sin, precision=precise)
    weights = spectral_weight.reshape(2, MODES, MODES, MODES, CH, CH)
    h_real = jnp.einsum("bijkc,ijkco->bijko", y_real, weights[0], precision=precise) - jnp.einsum("bijkc,ijkco->bijko", y_imag, weights[1], precision=precise)
    h_imag = jnp.einsum("bijkc,ijkco->bijko", y_real, weights[1], precision=precise) + jnp.einsum("bijkc,ijkco->bijko", y_imag, weights[0], precision=precise)
    q_real = jnp.einsum("bijko,yj->biyko", h_real, y_cos, precision=precise) - jnp.einsum("bijko,yj->biyko", h_imag, y_sin, precision=precise)
    q_imag = jnp.einsum("bijko,yj->biyko", h_real, y_sin, precision=precise) + jnp.einsum("bijko,yj->biyko", h_imag, y_cos, precision=precise)
    p_real = jnp.einsum("biyko,xi->bxyko", q_real, x_cos, precision=precise) - jnp.einsum("biyko,xi->bxyko", q_imag, x_sin, precision=precise)
    p_imag = jnp.einsum("biyko,xi->bxyko", q_real, x_sin, precision=precise) + jnp.einsum("biyko,xi->bxyko", q_imag, x_cos, precision=precise)
    factor = jnp.where(jnp.arange(MODES) == 0, 1.0, 2.0).astype(jnp.float32) / (NX * NY * NZ)
    inv_cos = z_cos * factor[None, :]
    inv_sin = z_sin * factor[None, :]

    def one_channel(channel):
        real_part = lax.dynamic_index_in_dim(p_real, channel, 4, keepdims=False)
        imag_part = lax.dynamic_index_in_dim(p_imag, channel, 4, keepdims=False)
        spectral = jnp.einsum("bxyk,zk->bxyz", real_part, inv_cos, precision=precise) - jnp.einsum("bxyk,zk->bxyz", imag_part, inv_sin, precision=precise)
        column = lax.dynamic_index_in_dim(pointwise_weight, channel, 1, keepdims=False)
        local = jnp.einsum("bcxyz,c->bxyz", field, column, precision=precise)
        shift = lax.dynamic_index_in_dim(channel_bias, channel, 0, keepdims=False)
        return jax.nn.gelu(spectral + local + shift, approximate=False)

    stacked = lax.map(one_channel, jnp.arange(CH, dtype=jnp.int32))
    return jnp.transpose(stacked, (1, 0, 2, 3, 4))
```

```python
import functools
import math

import jax
import jax.numpy as jnp
import ml_dtypes
import numpy as np
from jax import lax
from jax.experimental import pallas as pl
from jax.experimental.pallas import tpu as pltpu
from jax.sharding import PartitionSpec as P

MESH = pl.DeviceIdType.MESH
BF = jnp.bfloat16
F32 = jnp.float32
ANY = pl.BlockSpec(memory_space=pl.ANY)
VMEM = pl.BlockSpec(memory_space=pltpu.VMEM)

NX, NY, NZ, MODES, CH, G, H = 128, 128, 256, 32, 48, 16, 8
CT = CH // 16


def halves(table):
    high = table.astype(ml_dtypes.bfloat16)
    low = (table - high.astype(np.float64)).astype(ml_dtypes.bfloat16)
    return high, low


def signed(modes):
    number = np.arange(modes)
    return np.where(number < modes // 2, number, number - modes)


def angles(position, mode, length):
    return 2.0 * math.pi * ((position[:, None] * mode[None, :]) % length) / length


def lane_parts():
    lane = np.arange(128)
    return lane // 64, (lane // 32) % 2, (lane // 16) % 2, lane % 16


@functools.cache
def constants():
    ri, y2, k2, low = lane_parts()
    k = 2 * low + k2
    a = angles(np.arange(NZ), k, NZ)
    wave = np.where(ri[None, :] == 0, np.cos(a), -np.sin(a))
    forward = np.concatenate([wave * (y2 == 0), wave * (y2 == 1)], axis=0)
    tz = np.concatenate(halves(forward), axis=1)
    gain = np.where(k == 0, 1.0, 2.0) / (NX * NY * NZ)
    eh, el = halves((forward * gain).T)
    ez = np.concatenate([eh, eh], axis=0)
    f = signed(MODES)
    ax = angles(np.arange(NX), f, NX)
    ch, cl = halves(np.concatenate([np.cos(ax).T, np.sin(ax).T], axis=0))
    lx = np.concatenate(
        [np.concatenate([ch, ch], axis=1), np.concatenate([cl, np.zeros_like(cl)], axis=1)], axis=0
    )
    ch, cl = halves(np.concatenate([np.cos(ax), np.sin(ax)], axis=0))
    lix = np.concatenate([ch, ch, cl], axis=1)
    y = np.arange(NY).reshape(H, 2, 8)
    parts = [y[:, h].reshape(-1) for h in range(2)]
    ay = [angles(p, f, NY) for p in parts]
    rows = np.concatenate([t for q in ay for t in (np.cos(q).T, np.sin(q).T)], axis=0)
    ch, cl = halves(rows)
    ly = np.concatenate(
        [np.concatenate([ch, ch], axis=1), np.concatenate([cl, np.zeros_like(cl)], axis=1)], axis=0
    )
    rows = np.concatenate([np.cos(ay[0]), np.cos(ay[1]), np.sin(ay[0]), np.sin(ay[1])], axis=0)
    ch, cl = halves(rows)
    liy = np.concatenate([ch, ch, cl], axis=1)
    spread = np.zeros((128, 2, 2, 2, 8, CH))
    for half in range(2):
        for r in range(2):
            for q in range(2):
                for c in range(8):
                    spread[r * 64 + 32 + q * 16 + half * 8 + c, half, r, q, c, :] = 1.0
    spread = spread.reshape(128, -1)
    spread = np.concatenate([spread, spread], axis=0).astype(ml_dtypes.bfloat16)
    gather = np.zeros((2, 2, 8, CH, CT, 128))
    for q in range(2):
        for r in range(2):
            for o in range(CH):
                for h in range(2):
                    gather[q, r, :, o, o // 16, r * 64 + h * 32 + q * 16 + o % 16] = 1.0
    gather = gather.reshape(2 * 2 * 8 * CH, CT * 128).astype(ml_dtypes.bfloat16)
    return tz, lx, ly, spread, gather, liy, lix, ez, el


def split(value):
    high = value.astype(BF)
    return high, (value - high.astype(F32)).astype(BF)


def dot(a, b):
    return jnp.dot(a, b, preferred_element_type=F32)


def lanes16(tiles, lane):
    tiles = list(tiles)
    for bit in range(4):
        step = 1 << bit
        keep = (lane & step) == 0
        for index in range(16):
            if index & step:
                continue
            a, b = tiles[index], tiles[index | step]
            tiles[index] = jnp.where(keep, a, pltpu.roll(b, step, 1))
            tiles[index | step] = jnp.where(keep, pltpu.roll(a, 128 - step, 1), b)
    return tiles


def spectral_kernel(
    field, weight, spread, gather, tz, lx, ly, liy, lix, out,
    f_in, w_in, e_in, r_in, send1, recv1, send2, recv2, send3, recv3, send4, v_exp, h_acc, h_all,
    f_sem, w_sem, c_sem, s1, r1, s2, r2, s3, r3, s4, r4, o_sem,
):
    me, my = lax.axis_index("px"), lax.axis_index("py")

    def field_copy(t):
        return pltpu.make_async_copy(field.at[pl.ds(t * 16, 16)], f_in.at[pl.ds(t * 16, 16)], f_sem.at[t])

    def weight_copy(r, q):
        return pltpu.make_async_copy(weight.at[r, :, :, q, :], w_in.at[r, q], w_sem.at[r, q])

    const_copies = [
        pltpu.make_async_copy(spread, e_in, c_sem.at[0]),
        pltpu.make_async_copy(gather, r_in, c_sem.at[1]),
    ]
    for t in range(CT):
        field_copy(t).start()
    for copy in const_copies:
        copy.start()
    for r in range(2):
        for q in range(2):
            weight_copy(r, q).start()

    barrier = pltpu.get_barrier_semaphore()

    def greet_x(d, c):
        pl.semaphore_signal(barrier, inc=1, device_id=(lax.rem(me + d, G), my), device_id_type=MESH)
        return c

    def greet_y(d, c):
        pl.semaphore_signal(barrier, inc=1, device_id=(me, lax.rem(my + d, H)), device_id_type=MESH)
        return c

    lax.fori_loop(1, G, greet_x, 0)
    lax.fori_loop(1, H, greet_y, 0)
    pl.semaphore_wait(barrier, G + H - 2)

    def copy1(t, target, source):
        return pltpu.make_async_remote_copy(
            send1.at[t, target], recv1.at[t, pl.ds(source * 64, 64)], s1.at[t, target], r1.at[t, source],
            device_id=(target, my), device_id_type=MESH)

    def copy2(t, target, source):
        return pltpu.make_async_remote_copy(
            send2.at[t, pl.ds(target * 32, 32)], recv2.at[t, pl.ds(source * 32, 32)], s2.at[t, target],
            r2.at[t, source], device_id=(me, target), device_id_type=MESH)

    def copy3(t, target, source):
        return pltpu.make_async_remote_copy(
            send3.at[t, target], recv3.at[t, pl.ds(source * 32, 32)], s3.at[t, target], r3.at[t, source],
            device_id=(me, target), device_id_type=MESH)

    def copy4(t, target, source):
        return pltpu.make_async_remote_copy(
            send4.at[t, pl.ds(target * 64, 64)], out.at[t, source], s4.at[t, target], r4.at[t, source],
            device_id=(target, my), device_id_type=MESH)

    def send_all(copy, t, index, count):
        def body(d, c):
            copy(t, lax.rem(index + d, count), index).start()
            return c
        lax.fori_loop(1, count, body, 0)

    def wait_recv(copy, t, index, count):
        def body(d, c):
            peer = lax.rem(index + count - d, count)
            copy(t, peer, peer).wait_recv()
            return c
        lax.fori_loop(1, count, body, 0)

    def wait_send(copy, t, index, count):
        def body(d, c):
            copy(t, lax.rem(index + d, count), index).wait_send()
            return c
        lax.fori_loop(1, count, body, 0)

    lane = lax.broadcasted_iota(jnp.int32, (8, 128), 1)
    wide = lax.broadcasted_iota(jnp.int32, (1, 128), 1)
    sign = jnp.where(wide < 64, 1.0, -1.0).astype(F32)
    first = (wide & 32) == 0

    for t in range(CT):
        field_copy(t).wait()

        def z_step(xq, c, t=t):
            block = f_in[t * 16:(t + 1) * 16, pl.ds(xq * 4, 4)]
            rows = jnp.concatenate(
                [block[:, :, :8].reshape(512, NZ), block[:, :, 8:].reshape(512, NZ)], axis=1)
            high, low = split(rows)
            both = dot(high, tz[...])
            z = both[:, :128] + both[:, 128:] + dot(low, tz[:, :128])
            z = z.reshape(16, 4, 8, 128)
            for x in range(4):
                tiles = lanes16([z[c16, x] for c16 in range(16)], lane)
                for g in range(16):
                    send1[t, g, pl.ds(xq * 32 + x * 8, 8), :] = tiles[g]
            return c

        lax.fori_loop(0, 2, z_step, 0)
        send_all(copy1, t, me, G)
        recv1[t, pl.ds(me * 64, 64), :] = send1[t, me]

    for t in range(CT):
        wait_recv(copy1, t, me, G)
        for pair in range(4):
            data = jnp.concatenate(
                [recv1[t, pl.ds(2 * pair + h, 128, stride=8), :] for h in range(2)], axis=1)
            prod = dot(lx[...], jnp.concatenate(split(data), axis=0))
            prod = prod[:64] + prod[64:]
            for h in range(2):
                piece = prod[:, h * 128:(h + 1) * 128]
                send2[t, pl.ds(2 * pair + h, 32, stride=8), :] = piece[:32] + sign * pltpu.roll(piece[32:], 64, 1)
        send_all(copy2, t, my, H)
        recv2[t, pl.ds(my * 32, 32), :] = send2[t, pl.ds(my * 32, 32), :]

    for copy in const_copies:
        copy.wait()
    for t in range(CT):
        wait_recv(copy2, t, my, H)
        data = recv2[t].reshape(H, 4, 8, 128)
        data = jnp.concatenate([data[:, i].reshape(64, 128) for i in range(4)], axis=1)
        prod = dot(ly[...], jnp.concatenate(split(data), axis=0))
        prod = prod[:128] + prod[128:]
        rows = []
        for i in range(4):
            piece = prod[:, i * 128:(i + 1) * 128]
            u = jnp.where(first, piece[:32], piece[64:96])
            w = jnp.where(first, piece[32:64], piece[96:])
            v = u + sign * pltpu.roll(w, 64, 1)
            rows.append(v + pltpu.roll(v, 32, 1))
        v = jnp.concatenate(rows, axis=0)
        v_exp[t] = dot(jnp.concatenate(split(v), axis=1), e_in[...])

    for r in range(2):
        for q in range(2):
            weight_copy(r, q).wait()

    def mix(i, c):
        at = pl.ds(pl.multiple_of(i * 32, 32), 32)
        for q in range(2):
            for part in range(3):
                real = jnp.zeros((32, 128), F32)
                imag = jnp.zeros((32, 128), F32)
                for b in range(6):
                    base = (b % 2) * 4 * 384 + q * 384 + part * 128
                    vr = v_exp[b // 2, at, base:base + 128]
                    vi = v_exp[b // 2, at, base + 768:base + 768 + 128]
                    w0 = w_in[0, q, i, :, b * 384 + part * 128:b * 384 + part * 128 + 128]
                    w1 = w_in[1, q, i, :, b * 384 + part * 128:b * 384 + part * 128 + 128]
                    real += vr * w0 - vi * w1
                    imag += vr * w1 + vi * w0
                h_acc[at, q * 768 + part * 128:q * 768 + part * 128 + 128] = real
                h_acc[at, q * 768 + 384 + part * 128:q * 768 + 384 + part * 128 + 128] = imag
        return c

    lax.fori_loop(0, 4, mix, 0)
    high, low = split(h_acc[...])
    h_all[...] = dot(high, r_in[...]) + dot(low, r_in[...])

    for t in range(CT):
        data = jnp.concatenate(
            [h_all[i * 32:(i + 1) * 32, t * 128:(t + 1) * 128] for i in range(4)], axis=1)
        high, low = split(data)
        prod = dot(liy[...], jnp.concatenate([high, low, high], axis=0))
        for i in range(4):
            piece = prod[:, i * 128:(i + 1) * 128]
            a = jnp.where(first, piece[:64], piece[64:128])
            b = jnp.where(first, piece[128:192], piece[192:])
            q = a - sign * pltpu.roll(b, 64, 1)
            send3[t, :, i * 8:(i + 1) * 8, :] = q.reshape(H, 8, 128)
        send_all(copy3, t, my, H)
        recv3[t, pl.ds(my * 32, 32), :] = send3[t, my]

    for t in range(CT):
        wait_recv(copy3, t, my, H)
        for pair in range(4):
            data = jnp.concatenate(
                [recv3[t, pl.ds(2 * pair + h, 32, stride=8), :] for h in range(2)], axis=1)
            high, low = split(data)
            prod = dot(lix[...], jnp.concatenate([high, low, high], axis=0))
            for h in range(2):
                piece = prod[:, h * 128:(h + 1) * 128]
                send4[t, pl.ds(2 * pair + h, 128, stride=8), :] = piece[:128] - sign * pltpu.roll(piece[128:], 64, 1)
        send_all(copy4, t, me, G)
        pltpu.make_async_copy(send4.at[t, pl.ds(me * 64, 64)], out.at[t, me], o_sem.at[t]).start()

    for t in range(CT):
        wait_recv(copy4, t, me, G)
        pltpu.make_async_copy(send4.at[t, pl.ds(me * 64, 64)], out.at[t, me], o_sem.at[t]).wait()
        wait_send(copy1, t, me, G)
        wait_send(copy2, t, my, H)
        wait_send(copy3, t, my, H)
        wait_send(copy4, t, me, G)


def gelu(v):
    x = jnp.clip(v * math.sqrt(0.5), -3.832506856900711, 3.832506856900711)
    s = x * x
    top = jnp.full_like(s, 0.00022905065861350646)
    for a in (0.0034082910107109506, 0.050955695062380861, 0.18520832239976145, 1.128379143519084):
        top = top * s + a
    low = jnp.full_like(s, -1.1791602954361697e-7)
    for a in (0.000023547966471313185, 0.0010179625278914885, 0.014070470171167667, 0.11098505178285362,
              0.49746925110067538, 1.0):
        low = low * s + a
    return 0.5 * v * (1.0 + x * top / low)


def final_kernel(modes, field, point, bias, ez, el, out, a_high, a_low, shift):
    @pl.when(pl.program_id(0) == 0)
    def _():
        row = lax.broadcasted_iota(jnp.int32, (384, CH), 0)
        col = lax.broadcasted_iota(jnp.int32, (384, CH), 1)
        pick = (row // 8 == col)
        shift[...] = jnp.sum(jnp.where(pick, bias[...], 0.0), axis=1, keepdims=True) + jnp.zeros((384, 128), F32)
        picked = pick.astype(F32).astype(BF)
        r = lax.broadcasted_iota(jnp.int32, (384, 384), 0)
        c = lax.broadcasted_iota(jnp.int32, (384, 384), 1)
        same = (r % 8) == (c % 8)
        for piece, ref in zip(split(point[...]), (a_high, a_low)):
            wide = lax.dot_general(picked, piece, (((1,), (1,)), ((), ())), preferred_element_type=F32)
            full = lax.dot_general(wide.astype(BF), picked, (((1,), (1,)), ((), ())), preferred_element_type=F32)
            ref[...] = jnp.where(same, full, 0.0).astype(BF)

    lane = lax.broadcasted_iota(jnp.int32, (8, 128), 1)
    tiles = []
    for t in range(CT):
        tiles += lanes16([modes[t, s] for s in range(G)], lane)
    high, low = split(jnp.concatenate(tiles, axis=0))
    spectral = dot(jnp.concatenate([high, low], axis=1), ez[...]) + dot(high, el[...])
    for h in range(2):
        data = field[:, 0, h * 8:(h + 1) * 8, :].reshape(384, NZ)
        high, low = split(data)
        local = dot(a_high[...], high) + dot(a_low[...], high) + dot(a_high[...], low)
        total = spectral[:, h * NZ:(h + 1) * NZ] + local + shift[:, :1]
        out[:, 0, h * 8:(h + 1) * 8, :] = gelu(total).reshape(CH, 8, NZ)


def shards(field, spectral_weight, pointwise_weight, channel_bias):
    tz, lx, ly, spread, gather, liy, lix, ez, el = [jnp.asarray(c) for c in constants()]
    x_local = field.shape[2]
    field = field.reshape(field.shape[1:])
    scratch = [
        pltpu.VMEM((CH, 8, 16, NZ), F32),
        pltpu.VMEM((2, 2, 4, MODES, CH * CH), F32),
        pltpu.VMEM(spread.shape, BF),
        pltpu.VMEM(gather.shape, BF),
        pltpu.VMEM((CT, G, 64, 128), F32),
        pltpu.VMEM((CT, G * 64, 128), F32),
        pltpu.VMEM((CT, H * 32, 128), F32),
        pltpu.VMEM((CT, H * 32, 128), F32),
        pltpu.VMEM((CT, H, 32, 128), F32),
        pltpu.VMEM((CT, H * 32, 128), F32),
        pltpu.VMEM((CT, G * 64, 128), F32),
        pltpu.VMEM((CT, 128, 3072), F32),
        pltpu.VMEM((128, 1536), F32),
        pltpu.VMEM((128, 384), F32),
    ]
    dma = pltpu.SemaphoreType.DMA
    scratch += [dma((CT,)), dma((2, 2)), dma((2,))]
    scratch += [dma((CT, G)), dma((CT, G)), dma((CT, H)), dma((CT, H))]
    scratch += [dma((CT, H)), dma((CT, H)), dma((CT, G)), dma((CT, G)), dma((CT,))]
    modes = pl.pallas_call(
        spectral_kernel,
        out_shape=jax.ShapeDtypeStruct((CT, G, 64, 128), F32),
        in_specs=[ANY] * 4 + [VMEM] * 5,
        out_specs=ANY,
        scratch_shapes=scratch,
        compiler_params=pltpu.CompilerParams(
            collective_id=0, has_side_effects=True, vmem_limit_bytes=56 * 1024 * 1024),
        name="spectral",
    )(field, spectral_weight, spread, gather, tz, lx, ly, liy, lix)
    out = pl.pallas_call(
        final_kernel,
        grid=(x_local,),
        out_shape=jax.ShapeDtypeStruct(field.shape, F32),
        in_specs=[
            pl.BlockSpec((CT, G, 8, 128), lambda x: (0, 0, x, 0)),
            pl.BlockSpec((CH, 1, 16, NZ), lambda x: (0, x, 0, 0)),
            pl.BlockSpec((CH, CH), lambda x: (0, 0)),
            pl.BlockSpec((1, CH), lambda x: (0, 0)),
            pl.BlockSpec(ez.shape, lambda x: (0, 0)),
            pl.BlockSpec(el.shape, lambda x: (0, 0)),
        ],
        out_specs=pl.BlockSpec((CH, 1, 16, NZ), lambda x: (0, x, 0, 0)),
        scratch_shapes=[pltpu.VMEM((384, 384), BF), pltpu.VMEM((384, 384), BF), pltpu.VMEM((384, 128), F32)],
        compiler_params=pltpu.CompilerParams(vmem_limit_bytes=56 * 1024 * 1024),
        name="physical",
    )(modes, field, pointwise_weight, channel_bias.reshape(1, CH), ez, el)
    return out.reshape((1,) + out.shape)


def solution(mesh):
    in_specs = (P(None, None, "px", "py", None), P(None, "py", None, "px", None), P(), P())
    out_specs = P(None, None, "px", "py", None)
    return jax.shard_map(shards, mesh=mesh, in_specs=in_specs, out_specs=out_specs, check_vma=False)
```

```python
import functools
import math

import jax
import jax.numpy as jnp
import ml_dtypes
import numpy as np
from jax import lax
from jax.experimental import pallas as pl
from jax.experimental.pallas import tpu as pltpu
from jax.sharding import PartitionSpec as P

MESH = pl.DeviceIdType.MESH
BF = jnp.bfloat16
F32 = jnp.float32
ANY = pl.BlockSpec(memory_space=pl.ANY)
VMEM = pl.BlockSpec(memory_space=pltpu.VMEM)

NX, NY, NZ, MODES, CH, G, H = 128, 128, 256, 32, 48, 16, 8
CT = CH // 16
TA, TC, TB = range(3)


def halves(table):
    high = table.astype(ml_dtypes.bfloat16)
    low = (table - high.astype(np.float64)).astype(ml_dtypes.bfloat16)
    return high, low


def signed(modes):
    number = np.arange(modes)
    return np.where(number < modes // 2, number, number - modes)


def angles(position, mode, length):
    return 2.0 * math.pi * ((position[:, None] * mode[None, :]) % length) / length


def lane_parts():
    lane = np.arange(128)
    return lane // 64, (lane // 32) % 2, (lane // 16) % 2, lane % 16


@functools.cache
def constants():
    ri, y2, k2, low = lane_parts()
    k = 2 * low + k2
    a = angles(np.arange(NZ), k, NZ)
    wave = np.where(ri[None, :] == 0, np.cos(a), -np.sin(a))
    forward = np.concatenate([wave * (y2 == 0), wave * (y2 == 1)], axis=0)
    tz = np.concatenate(halves(forward), axis=1)
    gain = np.where(k == 0, 1.0, 2.0) / (NX * NY * NZ)
    eh, el = halves((forward * gain).T)
    ez = np.concatenate([eh, eh], axis=0)
    f = signed(MODES)
    ax = angles(np.arange(NX), f, NX)
    ch, cl = halves(np.concatenate([np.cos(ax).T, np.sin(ax).T], axis=0))
    lx = np.concatenate(
        [np.concatenate([ch, ch], axis=1), np.concatenate([cl, np.zeros_like(cl)], axis=1)], axis=0
    )
    ch, cl = halves(np.concatenate([np.cos(ax), np.sin(ax)], axis=0))
    lix = np.concatenate([ch, ch, cl], axis=1)
    y = np.arange(NY).reshape(H, 2, 8)
    parts = [y[:, h].reshape(-1) for h in range(2)]
    ay = [angles(p, f, NY) for p in parts]
    rows = np.concatenate([t for q in ay for t in (np.cos(q).T, np.sin(q).T)], axis=0)
    ch, cl = halves(rows)
    ly = np.concatenate(
        [np.concatenate([ch, ch], axis=1), np.concatenate([cl, np.zeros_like(cl)], axis=1)], axis=0
    )
    rows = np.concatenate([np.cos(ay[0]), np.cos(ay[1]), np.sin(ay[0]), np.sin(ay[1])], axis=0)
    ch, cl = halves(rows)
    liy = np.concatenate([ch, ch, cl], axis=1)
    pair = np.zeros((128, 4, 2, 8, CH))
    both = np.zeros((128, 2, 2, 2, 8, CH))
    for r in range(2):
        for c in range(32):
            pair[r * 64 + 32 + c, c // 8, r, c % 8, :] = 1.0
        for q in range(2):
            for c in range(16):
                both[r * 64 + 32 + q * 16 + c, c // 8, r, q, c % 8, :] = 1.0
    spread = np.stack([pair.reshape(128, -1), both.reshape(128, -1)])
    spread = np.concatenate([spread, spread], axis=1).astype(ml_dtypes.bfloat16)
    pair = np.zeros((2, 8, CH, 128))
    both = np.zeros((2, 2, 8, CH, 128))
    for r in range(2):
        for h in range(2):
            for o in range(32):
                pair[r, :, o, r * 64 + h * 32 + o] = 1.0
            for q in range(2):
                for o in range(16):
                    both[q, r, :, 32 + o, r * 64 + h * 32 + q * 16 + o] = 1.0
    gather = np.concatenate([pair.reshape(-1, 128), both.reshape(-1, 128)], axis=0).astype(ml_dtypes.bfloat16)
    return tz, lx, ly, spread, gather, liy, lix, ez, el


def split(value):
    high = value.astype(BF)
    return high, (value - high.astype(F32)).astype(BF)


def dot(a, b):
    return jnp.dot(a, b, preferred_element_type=F32)


def trade(a, b, step, lane):
    keep = (lane & step) == 0
    return jnp.where(keep, a, pltpu.roll(b, step, 1)), jnp.where(keep, pltpu.roll(a, 128 - step, 1), b)


def lanes16(tiles, lane):
    tiles = [pltpu.roll(tile, c, 1) if c else tile for c, tile in enumerate(tiles)]
    for bit in range(4):
        step = 1 << bit
        shift = (lane & step) != 0
        tiles = [jnp.where(shift, tiles[(h + step) % 16], tiles[h]) for h in range(16)]
    return [pltpu.roll(tiles[16 - g], 128 - g, 1) if g else tiles[0] for g in range(16)]


def gelu(v):
    return 0.5 * v * (1.0 + lax.erf(v * math.sqrt(0.5)))


def spectral_kernel(
    field, weight, spread, gather, ez, el, point, bias, tz, lx, ly, liy, lix, pre, last,
    f_in, w_in, e_in, r_in, ez_in, el_in, a_high, a_low, shift, held,
    send1, recv1, send2, recv2, send3, recv3, send4, recv4, v_exp, h_acc,
    f_sem, w_sem, c_sem, s1, r1, s2, r2, s3, r3, s4, r4, o_sem, p_sem,
):
    me, my = lax.axis_index("px"), lax.axis_index("py")

    def field_copy(t):
        return pltpu.make_async_copy(field.at[pl.ds(t * 16, 16)], f_in.at[pl.ds(t * 16, 16)], f_sem.at[t])

    def weight_copy(r, q):
        return pltpu.make_async_copy(weight.at[r, :, :, q, :], w_in.at[r, q], w_sem.at[r, q])

    const_copies = [
        pltpu.make_async_copy(spread, e_in, c_sem.at[0]),
        pltpu.make_async_copy(gather, r_in, c_sem.at[1]),
        pltpu.make_async_copy(ez, ez_in, c_sem.at[2]),
        pltpu.make_async_copy(el, el_in, c_sem.at[3]),
    ]
    for t in (2, 0, 1):
        field_copy(t).start()

    barrier = pltpu.get_barrier_semaphore()

    def greet_x(d, c):
        pl.semaphore_signal(barrier, inc=1, device_id=(lax.rem(me + d, G), my), device_id_type=MESH)
        return c

    def greet_y(d, c):
        pl.semaphore_signal(barrier, inc=1, device_id=(me, lax.rem(my + d, H)), device_id_type=MESH)
        return c

    lax.fori_loop(1, G, greet_x, 0)
    lax.fori_loop(1, H, greet_y, 0)

    def copy1(part, half, target, source):
        tiles, sem = (pl.ds(TB, 1), 1) if part else (pl.ds(TA, 2), 0)
        return pltpu.make_async_remote_copy(
            send1.at[tiles, target, pl.ds(half * 32, 32)], recv1.at[tiles, pl.ds(source * 64 + half * 32, 32)],
            s1.at[sem], r1.at[sem], device_id=(target, my), device_id_type=MESH)

    def send1_all(part, half):
        def body(d, c):
            copy1(part, half, lax.rem(me + d, G), me).start()
            return c
        lax.fori_loop(1, G, body, 0)

    def copy2(t, target, source):
        return pltpu.make_async_remote_copy(
            send2.at[t, pl.ds(target * 32, 32)], recv2.at[t, pl.ds(source * 32, 32)], s2.at[t],
            r2.at[t], device_id=(me, target), device_id_type=MESH)

    def copy3(t, target, source):
        return pltpu.make_async_remote_copy(
            send3.at[t, target], recv3.at[t, pl.ds(source * 32, 32)], s3.at[t], r3.at[t],
            device_id=(me, target), device_id_type=MESH)

    def copy4(t, target, source):
        return pltpu.make_async_remote_copy(
            send4.at[t, pl.ds(target * 64, 64)], recv4.at[t, source], s4.at[t], r4.at[t],
            device_id=(target, my), device_id_type=MESH)

    def send_all(copy, t, index, count):
        def body(d, c):
            copy(t, lax.rem(index + d, count), index).start()
            return c
        lax.fori_loop(1, count, body, 0)

    def all1(part):
        tiles = pl.ds(TB, 1) if part else pl.ds(TA, 2)
        return pltpu.make_async_remote_copy(
            send1.at[tiles, pl.ds(0, G - 1)], recv1.at[tiles, pl.ds(0, (G - 1) * 64)], s1.at[part], r1.at[part],
            device_id=(lax.rem(me + 1, G), my), device_id_type=MESH)

    def all2(t):
        return pltpu.make_async_remote_copy(
            send2.at[t, pl.ds(0, (H - 1) * 32)], recv2.at[t, pl.ds(0, (H - 1) * 32)], s2.at[t], r2.at[t],
            device_id=(me, lax.rem(my + 1, H)), device_id_type=MESH)

    def all3(t):
        return pltpu.make_async_remote_copy(
            send3.at[t, pl.ds(0, H - 1)], recv3.at[t, pl.ds(0, (H - 1) * 32)], s3.at[t], r3.at[t],
            device_id=(me, lax.rem(my + 1, H)), device_id_type=MESH)

    def all4(t):
        return pltpu.make_async_remote_copy(
            send4.at[t, pl.ds(0, (G - 1) * 64)], recv4.at[t, pl.ds(0, G - 1)], s4.at[t], r4.at[t],
            device_id=(lax.rem(me + 1, G), my), device_id_type=MESH)

    lane = lax.broadcasted_iota(jnp.int32, (8, 128), 1)
    wide = lax.broadcasted_iota(jnp.int32, (1, 128), 1)
    sign = jnp.where(wide < 64, 1.0, -1.0).astype(F32)
    first = (wide & 32) == 0

    def z_tiles(first_c, count, x, xs):
        block = f_in[first_c:first_c + count, pl.ds(x, xs)]
        rows = jnp.concatenate(
            [block[:, :, :8].reshape(count * xs * 8, NZ), block[:, :, 8:].reshape(count * xs * 8, NZ)], axis=1)
        high, low = split(rows)
        prod = dot(high, tz[...])
        z = (prod[:, :128] + prod[:, 128:] + dot(low, tz[:, :128])).reshape(count, xs, 8, 128)
        return [[lanes16([z[g * 16 + c, q] for c in range(16)], lane) for g in range(count // 16)] for q in range(xs)]

    def z_both(xq, c):
        for q, (tiles,) in enumerate(z_tiles(32, 16, xq * 4, 4)):
            for g in range(G):
                send1[TB, g, pl.ds(xq * 32 + q * 8, 8), :] = tiles[g]
        return c

    def z_pair(xq, c):
        for q, (even, odd) in enumerate(z_tiles(0, 32, xq * 2, 2)):
            for g in range(G):
                a, b = trade(even[g], odd[g], 16, lane)
                send1[TA, g, pl.ds(xq * 16 + q * 8, 8), :] = a
                send1[TC, g, pl.ds(xq * 16 + q * 8, 8), :] = b
        return c

    field_copy(2).wait()
    z_both(0, 0)
    pl.semaphore_wait(barrier, G + H - 2)
    send1_all(1, 0)
    z_both(1, 0)
    send1_all(1, 1)
    field_copy(0).wait()
    field_copy(1).wait()
    for half in range(2):
        lax.fori_loop(half * 2, half * 2 + 2, z_pair, 0)
        send1_all(0, half)
    for t in range(CT):
        recv1[t, pl.ds(me * 64, 64), :] = send1[t, me]

    for copy in const_copies:
        copy.start()
    for r in range(2):
        for q in range(2):
            weight_copy(r, q).start()

    row = lax.broadcasted_iota(jnp.int32, (384, CH), 0)
    col = lax.broadcasted_iota(jnp.int32, (384, CH), 1)
    pick = row // 8 == col
    shift[...] = jnp.sum(jnp.where(pick, bias[...], 0.0), axis=1, keepdims=True) + jnp.zeros((384, 128), F32)
    picked = pick.astype(F32).astype(BF)
    row = lax.broadcasted_iota(jnp.int32, (384, 384), 0)
    col = lax.broadcasted_iota(jnp.int32, (384, 384), 1)
    same = (row % 8) == (col % 8)
    for piece, ref in zip(split(point[...]), (a_high, a_low)):
        tall = lax.dot_general(picked, piece, (((1,), (1,)), ((), ())), preferred_element_type=F32)
        full = lax.dot_general(tall.astype(BF), picked, (((1,), (1,)), ((), ())), preferred_element_type=F32)
        ref[...] = jnp.where(same, full, 0.0).astype(BF)

    def local_step(x, c):
        for h in range(2):
            high, low = split(f_in[:, x, h * 8:(h + 1) * 8, :].reshape(384, NZ))
            local = dot(a_high[...], high) + dot(a_low[...], high) + dot(a_high[...], low) + shift[:, :1]
            held[:, x, h * 8:(h + 1) * 8, :] = local.reshape(CH, 8, NZ)
        return c

    lax.fori_loop(0, 8, local_step, 0)

    def pre_copy(t):
        return pltpu.make_async_copy(held.at[pl.ds(t * 16, 16)], pre.at[pl.ds(t * 16, 16)], p_sem.at[t])

    def along_x(t):
        for pair in range(4):
            data = jnp.concatenate(
                [recv1[t, pl.ds(2 * pair + h, 128, stride=8), :] for h in range(2)], axis=1)
            prod = dot(lx[...], jnp.concatenate(split(data), axis=0))
            prod = prod[:64] + prod[64:]
            for h in range(2):
                piece = prod[:, h * 128:(h + 1) * 128]
                send2[t, pl.ds(2 * pair + h, 32, stride=8), :] = piece[:32] + sign * pltpu.roll(piece[32:], 64, 1)
        send_all(copy2, t, my, H)
        recv2[t, pl.ds(my * 32, 32), :] = send2[t, pl.ds(my * 32, 32), :]

    def along_y(t):
        all2(t).wait_recv()
        data = recv2[t].reshape(H, 4, 8, 128)
        data = jnp.concatenate([data[:, i].reshape(64, 128) for i in range(4)], axis=1)
        prod = dot(ly[...], jnp.concatenate(split(data), axis=0))
        prod = prod[:128] + prod[128:]
        rows = []
        for i in range(4):
            piece = prod[:, i * 128:(i + 1) * 128]
            u = jnp.where(first, piece[:32], piece[64:96])
            w = jnp.where(first, piece[32:64], piece[96:])
            v = u + sign * pltpu.roll(w, 64, 1)
            rows.append(v + pltpu.roll(v, 32, 1))
        v = jnp.concatenate(rows, axis=0)
        v_exp[t] = dot(jnp.concatenate(split(v), axis=1), e_in[1 if t == TB else 0])

    def mix(q):
        t = (TA, TC)[q]

        def body(i, c):
            at = pl.ds(pl.multiple_of(i * 32, 32), 32)
            for part in range(3):
                real = jnp.zeros((32, 128), F32)
                imag = jnp.zeros((32, 128), F32)
                for b in range(6):
                    col = b * 384 + part * 128
                    if b < 4:
                        source, base, gap = t, b * 768 + part * 128, 384
                    else:
                        source, base, gap = TB, (b - 4) * 1536 + q * 384 + part * 128, 768
                    vr = v_exp[source, at, base:base + 128]
                    vi = v_exp[source, at, base + gap:base + gap + 128]
                    w0 = w_in[0, q, i, :, col:col + 128]
                    w1 = w_in[1, q, i, :, col:col + 128]
                    real += vr * w0 - vi * w1
                    imag += vr * w1 + vi * w0
                col = q * 768 + part * 128
                h_acc[at, col:col + 128] = real
                h_acc[at, col + 384:col + 384 + 128] = imag
            return c

        lax.fori_loop(0, 4, body, 0)

    def collect(t):
        if t == TB:
            source, table = h_acc[...], r_in[768:, :]
        else:
            source, table = h_acc[:, (0 if t == TA else 768):(768 if t == TA else 1536)], r_in[:768, :]
        high, low = split(source)
        return dot(high, table) + dot(low, table)

    def back_y(t):
        h_all = collect(t)
        data = jnp.concatenate([h_all[i * 32:(i + 1) * 32] for i in range(4)], axis=1)
        high, low = split(data)
        prod = dot(liy[...], jnp.concatenate([high, low, high], axis=0))
        for i in range(4):
            piece = prod[:, i * 128:(i + 1) * 128]
            a = jnp.where(first, piece[:64], piece[64:128])
            b = jnp.where(first, piece[128:192], piece[192:])
            q = a - sign * pltpu.roll(b, 64, 1)
            send3[t, :, i * 8:(i + 1) * 8, :] = q.reshape(H, 8, 128)
        send_all(copy3, t, my, H)
        recv3[t, pl.ds(my * 32, 32), :] = send3[t, my]

    def back_x(t):
        all3(t).wait_recv()
        for pair in range(4):
            data = jnp.concatenate(
                [recv3[t, pl.ds(2 * pair + h, 32, stride=8), :] for h in range(2)], axis=1)
            high, low = split(data)
            prod = dot(lix[...], jnp.concatenate([high, low, high], axis=0))
            for h in range(2):
                piece = prod[:, h * 128:(h + 1) * 128]
                send4[t, pl.ds(2 * pair + h, 128, stride=8), :] = piece[:128] - sign * pltpu.roll(piece[128:], 64, 1)
        send_all(copy4, t, me, G)
        recv4[t, me] = send4[t, pl.ds(me * 64, 64), :]

    pre_copy(CT - 1).start()
    all1(1).wait_recv()
    along_x(TB)
    all1(0).wait_recv()
    along_x(TA)
    along_x(TC)
    for copy in const_copies:
        copy.wait()
    for r in range(2):
        for q in range(2):
            weight_copy(r, q).wait()
    along_y(TB)
    along_y(TA)
    mix(0)
    back_y(TA)
    along_y(TC)
    mix(1)
    back_y(TC)
    back_y(TB)
    back_x(TA)
    back_x(TC)
    back_x(TB)

    all1(0).wait_send()
    all1(1).wait_send()
    for t in range(CT):
        all2(t).wait_send()
        all3(t).wait_send()
    all4(TA).wait_recv()
    all4(TC).wait_recv()

    def finish(xq, c):
        tiles = []
        for x in range(2):
            at = pl.ds(xq * 16 + x * 8, 8)
            even = lanes16([recv4[TA, s, at, :] for s in range(G)], lane)
            odd = lanes16([recv4[TC, s, at, :] for s in range(G)], lane)
            tiles.append([trade(a, b, 16, lane) for a, b in zip(even, odd)])
        rows = jnp.concatenate([tiles[x][o][p] for p in range(2) for o in range(16) for x in range(2)], axis=0)
        high, low = split(rows)
        spectral = dot(jnp.concatenate([high, low], axis=1), ez_in[...]) + dot(high, el_in[...])
        for h in range(2):
            at = (pl.ds(0, 32), pl.ds(xq * 2, 2), pl.ds(h * 8, 8), slice(None))
            held[at] = gelu(held[at] + spectral[:, h * NZ:(h + 1) * NZ].reshape(32, 2, 8, NZ))
        return c

    lax.fori_loop(0, 4, finish, 0)
    for t in range(CT - 1):
        pre_copy(t).start()
    for t in range(CT):
        all4(t).wait_send()
    all4(TB).wait_recv()
    copy = pltpu.make_async_copy(recv4.at[TB], last, o_sem)
    copy.start()
    copy.wait()
    for t in range(CT):
        pre_copy(t).wait()


def final_kernel(pre, modes, ez, el, out, through, work, m_in, ez_in, el_in, t_sem, w_sem, o_sem, v_sem, c_sem):
    lane = lax.broadcasted_iota(jnp.int32, (8, 128), 1)
    done = CH - 16
    small = [
        pltpu.make_async_copy(modes, m_in, c_sem.at[0]),
        pltpu.make_async_copy(ez, ez_in, c_sem.at[1]),
        pltpu.make_async_copy(el, el_in, c_sem.at[2]),
    ]
    load = [pltpu.make_async_copy(pre.at[pl.ds(done, 16), pl.ds(2 * p, 2)], work.at[p], w_sem.at[p]) for p in range(4)]
    store = [pltpu.make_async_copy(work.at[p], out.at[pl.ds(done, 16), pl.ds(2 * p, 2)], v_sem.at[p]) for p in range(4)]
    take = [pltpu.make_async_copy(pre.at[pl.ds(8 * p, 8)], through.at[p], t_sem.at[p]) for p in range(4)]
    give = [pltpu.make_async_copy(through.at[p], out.at[pl.ds(8 * p, 8)], o_sem.at[p]) for p in range(4)]
    for copy in small + load[:1] + take[:1] + load[1:] + take[1:]:
        copy.start()
    for copy in small:
        copy.wait()
    for p in range(4):
        load[p].wait()
        tiles = [lanes16([m_in[s, p * 16 + x * 8:p * 16 + (x + 1) * 8, :] for s in range(G)], lane) for x in range(2)]
        high, low = split(jnp.concatenate([tile[o] for o in range(16) for tile in tiles], axis=0))
        spectral = dot(jnp.concatenate([high, low], axis=1), ez_in[...]) + dot(high, el_in[...])
        for h in range(2):
            at = (p, slice(None), slice(None), slice(h * 8, (h + 1) * 8), slice(None))
            work[at] = gelu(work[at] + spectral[:, h * NZ:(h + 1) * NZ].reshape(16, 2, 8, NZ))
        store[p].start()
        take[p].wait()
        give[p].start()
    for copy in store + give:
        copy.wait()


def shards(field, spectral_weight, pointwise_weight, channel_bias):
    tz, lx, ly, spread, gather, liy, lix, ez, el = [jnp.asarray(c) for c in constants()]
    field = field.reshape(field.shape[1:])
    scratch = [
        pltpu.VMEM((CH, 8, 16, NZ), F32),
        pltpu.VMEM((2, 2, 4, MODES, CH * CH), F32),
        pltpu.VMEM(spread.shape, BF),
        pltpu.VMEM(gather.shape, BF),
        pltpu.VMEM(ez.shape, BF),
        pltpu.VMEM(el.shape, BF),
        pltpu.VMEM((384, 384), BF),
        pltpu.VMEM((384, 384), BF),
        pltpu.VMEM((384, 128), F32),
        pltpu.VMEM((CH, 8, 16, NZ), F32),
        pltpu.VMEM((CT, G, 64, 128), F32),
        pltpu.VMEM((CT, G * 64, 128), F32),
        pltpu.VMEM((CT, H * 32, 128), F32),
        pltpu.VMEM((CT, H * 32, 128), F32),
        pltpu.VMEM((CT, H, 32, 128), F32),
        pltpu.VMEM((CT, H * 32, 128), F32),
        pltpu.VMEM((CT, G * 64, 128), F32),
        pltpu.VMEM((CT, G, 64, 128), F32),
        pltpu.VMEM((CT, 128, 3072), F32),
        pltpu.VMEM((128, 1536), F32),
    ]
    dma = pltpu.SemaphoreType.DMA
    scratch += [dma((CT,)), dma((2, 2)), dma((4,))]
    scratch += [dma((CT,))] * 8 + [dma, dma((CT,))]
    pre, last = pl.pallas_call(
        spectral_kernel,
        out_shape=[jax.ShapeDtypeStruct(field.shape, F32), jax.ShapeDtypeStruct((G, 64, 128), F32)],
        in_specs=[ANY] * 6 + [VMEM] * 7,
        out_specs=[ANY] * 2,
        scratch_shapes=scratch,
        compiler_params=pltpu.CompilerParams(
            collective_id=0, has_side_effects=True, vmem_limit_bytes=60 * 1024 * 1024),
        name="spectral",
    )(field, spectral_weight, spread, gather, ez, el, pointwise_weight, channel_bias.reshape(1, CH),
      tz, lx, ly, liy, lix)
    out = pl.pallas_call(
        final_kernel,
        out_shape=jax.ShapeDtypeStruct(field.shape, F32),
        in_specs=[ANY] * 4,
        out_specs=ANY,
        scratch_shapes=[
            pltpu.VMEM((4, 8, 8, 16, NZ), F32),
            pltpu.VMEM((4, 16, 2, 16, NZ), F32),
            pltpu.VMEM((G, 64, 128), F32),
            pltpu.VMEM(ez.shape, BF),
            pltpu.VMEM(el.shape, BF),
            dma((4,)), dma((4,)), dma((4,)), dma((4,)), dma((3,)),
        ],
        compiler_params=pltpu.CompilerParams(vmem_limit_bytes=60 * 1024 * 1024),
        name="physical",
    )(pre, last, ez, el)
    return out.reshape((1,) + out.shape)


def solution(mesh):
    in_specs = (P(None, None, "px", "py", None), P(None, "py", None, "px", None), P(), P())
    out_specs = P(None, None, "px", "py", None)
    return jax.shard_map(shards, mesh=mesh, in_specs=in_specs, out_specs=out_specs, check_vma=False)
```

```python
import functools
import math

import jax
import jax.numpy as jnp
import ml_dtypes
import numpy as np
from jax import lax
from jax.experimental import pallas as pl
from jax.experimental.pallas import tpu as pltpu
from jax.sharding import PartitionSpec as P

MESH = pl.DeviceIdType.MESH
BF = jnp.bfloat16
F32 = jnp.float32
ANY = pl.BlockSpec(memory_space=pl.ANY)
VMEM = pl.BlockSpec(memory_space=pltpu.VMEM)

NX, NY, NZ, MODES, CH, G, H = 128, 128, 256, 32, 48, 16, 8
CT = CH // 16
TA, TC, TB = range(3)


def halves(table):
    high = table.astype(ml_dtypes.bfloat16)
    low = (table - high.astype(np.float64)).astype(ml_dtypes.bfloat16)
    return high, low


def signed(modes):
    number = np.arange(modes)
    return np.where(number < modes // 2, number, number - modes)


def angles(position, mode, length):
    return 2.0 * math.pi * ((position[:, None] * mode[None, :]) % length) / length


def lane_parts():
    lane = np.arange(128)
    return lane // 64, (lane // 32) % 2, (lane // 16) % 2, lane % 16


@functools.cache
def constants():
    ri, y2, k2, low = lane_parts()
    k = 2 * low + k2
    a = angles(np.arange(NZ), k, NZ)
    wave = np.where(ri[None, :] == 0, np.cos(a), -np.sin(a))
    forward = np.concatenate([wave * (y2 == 0), wave * (y2 == 1)], axis=0)
    tz = np.concatenate(halves(forward), axis=1)
    gain = np.where(k == 0, 1.0, 2.0) / (NX * NY * NZ)
    eh, el = halves((forward * gain).T)
    ez = np.concatenate([eh, eh], axis=0)
    f = signed(MODES)
    ax = angles(np.arange(NX), f, NX)
    ch, cl = halves(np.concatenate([np.cos(ax).T, np.sin(ax).T], axis=0))
    lx = np.concatenate(
        [np.concatenate([ch, ch], axis=1), np.concatenate([cl, np.zeros_like(cl)], axis=1)], axis=0
    )
    ch, cl = halves(np.concatenate([np.cos(ax), np.sin(ax)], axis=0))
    lix = np.concatenate([ch, ch, cl], axis=1)
    y = np.arange(NY).reshape(H, 2, 8)
    parts = [y[:, h].reshape(-1) for h in range(2)]
    ay = [angles(p, f, NY) for p in parts]
    rows = np.concatenate([t for q in ay for t in (np.cos(q).T, np.sin(q).T)], axis=0)
    ch, cl = halves(rows)
    ly = np.concatenate(
        [np.concatenate([ch, ch], axis=1), np.concatenate([cl, np.zeros_like(cl)], axis=1)], axis=0
    )
    rows = np.concatenate([np.cos(ay[0]), np.cos(ay[1]), np.sin(ay[0]), np.sin(ay[1])], axis=0)
    ch, cl = halves(rows)
    liy = np.concatenate([ch, ch, cl], axis=1)
    pair = np.zeros((128, 4, 2, 8, CH))
    both = np.zeros((128, 2, 2, 2, 8, CH))
    for r in range(2):
        for c in range(32):
            pair[r * 64 + 32 + c, c // 8, r, c % 8, :] = 1.0
        for q in range(2):
            for c in range(16):
                both[r * 64 + 32 + q * 16 + c, c // 8, r, q, c % 8, :] = 1.0
    spread = np.stack([pair.reshape(128, -1), both.reshape(128, -1)])
    spread = np.concatenate([spread, spread], axis=1).astype(ml_dtypes.bfloat16)
    pair = np.zeros((2, 8, CH, 128))
    both = np.zeros((2, 2, 8, CH, 128))
    for r in range(2):
        for h in range(2):
            for o in range(32):
                pair[r, :, o, r * 64 + h * 32 + o] = 1.0
            for q in range(2):
                for o in range(16):
                    both[q, r, :, 32 + o, r * 64 + h * 32 + q * 16 + o] = 1.0
    gather = np.concatenate([pair.reshape(-1, 128), both.reshape(-1, 128)], axis=0).astype(ml_dtypes.bfloat16)
    return tz, lx, ly, spread, gather, liy, lix, ez, el


def split(value):
    high = value.astype(BF)
    return high, (value - high.astype(F32)).astype(BF)


def dot(a, b):
    return jnp.dot(a, b, preferred_element_type=F32)


def trade(a, b, step, lane):
    keep = (lane & step) == 0
    return jnp.where(keep, a, pltpu.roll(b, step, 1)), jnp.where(keep, pltpu.roll(a, 128 - step, 1), b)


def lanes16(tiles, lane):
    tiles = [pltpu.roll(tile, c, 1) if c else tile for c, tile in enumerate(tiles)]
    for bit in range(4):
        step = 1 << bit
        shift = (lane & step) != 0
        tiles = [jnp.where(shift, tiles[(h + step) % 16], tiles[h]) for h in range(16)]
    return [pltpu.roll(tiles[16 - g], 128 - g, 1) if g else tiles[0] for g in range(16)]


def gelu(v):
    return 0.5 * v * (1.0 + lax.erf(v * math.sqrt(0.5)))


def spectral_kernel(
    field, weight, spread, gather, ez, el, point_far, bias_far, tz_far, lx_far, ly_far, liy_far, lix_far, held, last,
    f_in, w_in, e_in, r_in, ez_in, el_in, tz, lx, ly, liy, lix, point, bias, a_high, a_low, shift,
    send1, recv1, send2, recv2, send3, recv3, send4, recv4, v_exp, h_acc,
    f_sem, w_sem, c_sem, s1, r1, s2, r2, s3, r3, s4, r4, o_sem,
):
    me, my = lax.axis_index("px"), lax.axis_index("py")

    def field_copy(t):
        return pltpu.make_async_copy(field.at[pl.ds(t * 16, 16)], f_in.at[pl.ds(t * 16, 16)], f_sem.at[t])

    def weight_copy(r, q):
        return pltpu.make_async_copy(weight.at[r, :, :, q, :], w_in.at[r, q], w_sem.at[r, q])

    const_copies = [
        pltpu.make_async_copy(spread, e_in, c_sem.at[0]),
        pltpu.make_async_copy(gather, r_in, c_sem.at[1]),
        pltpu.make_async_copy(ez, ez_in, c_sem.at[2]),
        pltpu.make_async_copy(el, el_in, c_sem.at[3]),
        pltpu.make_async_copy(lx_far, lx, c_sem.at[4]),
        pltpu.make_async_copy(ly_far, ly, c_sem.at[5]),
        pltpu.make_async_copy(liy_far, liy, c_sem.at[6]),
        pltpu.make_async_copy(lix_far, lix, c_sem.at[7]),
    ]
    conv_copies = [
        pltpu.make_async_copy(point_far, point, c_sem.at[9]),
        pltpu.make_async_copy(bias_far, bias, c_sem.at[10]),
    ]
    first_table = pltpu.make_async_copy(tz_far, tz, c_sem.at[8])
    first_table.start()
    for t in (2, 0, 1):
        field_copy(t).start()

    barrier = pltpu.get_barrier_semaphore()

    def greet_x(d, c):
        pl.semaphore_signal(barrier, inc=1, device_id=(lax.rem(me + d, G), my), device_id_type=MESH)
        return c

    def greet_y(d, c):
        pl.semaphore_signal(barrier, inc=1, device_id=(me, lax.rem(my + d, H)), device_id_type=MESH)
        return c

    lax.fori_loop(1, G, greet_x, 0)
    lax.fori_loop(1, H, greet_y, 0)

    def copy1(t, first_row, rows, target, source):
        return pltpu.make_async_remote_copy(
            send1.at[t, target, pl.ds(first_row, rows)], recv1.at[t, pl.ds(source * 64 + first_row, rows)],
            s1.at[t], r1.at[t], device_id=(target, my), device_id_type=MESH)

    def send1_all(t, first_row, rows):
        def body(d, c):
            copy1(t, first_row, rows, lax.rem(me + d, G), me).start()
            return c
        lax.fori_loop(1, G, body, 0)

    def copy2(t, target, source):
        return pltpu.make_async_remote_copy(
            send2.at[t, pl.ds(target * 32, 32)], recv2.at[t, pl.ds(source * 32, 32)], s2.at[t],
            r2.at[t], device_id=(me, target), device_id_type=MESH)

    def copy3(t, target, source):
        return pltpu.make_async_remote_copy(
            send3.at[t, target], recv3.at[t, pl.ds(source * 32, 32)], s3.at[t], r3.at[t],
            device_id=(me, target), device_id_type=MESH)

    def landing(t):
        return last if t == TB else recv4.at[t]

    def copy4(t, target, source):
        return pltpu.make_async_remote_copy(
            send4.at[t, pl.ds(target * 64, 64)], landing(t).at[source], s4.at[t], r4.at[t],
            device_id=(target, my), device_id_type=MESH)

    def own4():
        return pltpu.make_async_copy(send4.at[TB, pl.ds(me * 64, 64)], last.at[me], o_sem)

    def send_all(copy, t, index, count):
        def body(d, c):
            copy(t, lax.rem(index + d, count), index).start()
            return c
        lax.fori_loop(1, count, body, 0)

    def all1(t):
        return pltpu.make_async_remote_copy(
            send1.at[t, pl.ds(0, G - 1)], recv1.at[t, pl.ds(0, (G - 1) * 64)], s1.at[t], r1.at[t],
            device_id=(lax.rem(me + 1, G), my), device_id_type=MESH)

    def all2(t):
        return pltpu.make_async_remote_copy(
            send2.at[t, pl.ds(0, (H - 1) * 32)], recv2.at[t, pl.ds(0, (H - 1) * 32)], s2.at[t], r2.at[t],
            device_id=(me, lax.rem(my + 1, H)), device_id_type=MESH)

    def all3(t):
        return pltpu.make_async_remote_copy(
            send3.at[t, pl.ds(0, H - 1)], recv3.at[t, pl.ds(0, (H - 1) * 32)], s3.at[t], r3.at[t],
            device_id=(me, lax.rem(my + 1, H)), device_id_type=MESH)

    def all4(t):
        return pltpu.make_async_remote_copy(
            send4.at[t, pl.ds(0, (G - 1) * 64)], landing(t).at[pl.ds(0, G - 1)], s4.at[t], r4.at[t],
            device_id=(lax.rem(me + 1, G), my), device_id_type=MESH)

    lane = lax.broadcasted_iota(jnp.int32, (8, 128), 1)
    wide = lax.broadcasted_iota(jnp.int32, (1, 128), 1)
    sign = jnp.where(wide < 64, 1.0, -1.0).astype(F32)
    first = (wide & 32) == 0

    def z_tiles(first_c, count, x, xs):
        block = f_in[first_c:first_c + count, pl.ds(x, xs)]
        rows = jnp.concatenate(
            [block[:, :, :8].reshape(count * xs * 8, NZ), block[:, :, 8:].reshape(count * xs * 8, NZ)], axis=1)
        high, low = split(rows)
        prod = dot(high, tz[...])
        z = (prod[:, :128] + prod[:, 128:] + dot(low, tz[:, :128])).reshape(count, xs, 8, 128)
        return [[lanes16([z[g * 16 + c, q] for c in range(16)], lane) for g in range(count // 16)] for q in range(xs)]

    def z_both(xq, c):
        for q, (tiles,) in enumerate(z_tiles(32, 16, xq * 4, 4)):
            for g in range(G):
                send1[TB, g, pl.ds(xq * 32 + q * 8, 8), :] = tiles[g]
        return c

    def z_pair(xq, c):
        for q, (even, odd) in enumerate(z_tiles(0, 32, xq * 2, 2)):
            for g in range(G):
                a, b = trade(even[g], odd[g], 16, lane)
                send1[TA, g, pl.ds(xq * 16 + q * 8, 8), :] = a
                send1[TC, g, pl.ds(xq * 16 + q * 8, 8), :] = b
        return c

    first_table.wait()
    field_copy(2).wait()
    z_both(0, 0)
    pl.semaphore_wait(barrier, G + H - 2)
    send1_all(TB, 0, 32)
    for copy in conv_copies:
        copy.start()
    z_both(1, 0)
    send1_all(TB, 32, 32)
    field_copy(0).wait()
    field_copy(1).wait()
    for half in range(2):
        lax.fori_loop(half * 2, half * 2 + 2, z_pair, 0)
        send1_all(TA, half * 32, 32)
    send1_all(TC, 0, 64)
    for t in range(CT):
        recv1[t, pl.ds(me * 64, 64), :] = send1[t, me]

    for copy in const_copies:
        copy.start()
    for r in range(2):
        for q in range(2):
            weight_copy(r, q).start()

    for copy in conv_copies:
        copy.wait()
    row = lax.broadcasted_iota(jnp.int32, (384, CH), 0)
    col = lax.broadcasted_iota(jnp.int32, (384, CH), 1)
    pick = row // 8 == col
    shift[...] = jnp.sum(jnp.where(pick, bias[...], 0.0), axis=1, keepdims=True) + jnp.zeros((384, 128), F32)
    picked = pick.astype(F32).astype(BF)
    row = lax.broadcasted_iota(jnp.int32, (384, 384), 0)
    col = lax.broadcasted_iota(jnp.int32, (384, 384), 1)
    same = (row % 8) == (col % 8)
    for piece, ref in zip(split(point[...]), (a_high, a_low)):
        tall = lax.dot_general(picked, piece, (((1,), (1,)), ((), ())), preferred_element_type=F32)
        full = lax.dot_general(tall.astype(BF), picked, (((1,), (1,)), ((), ())), preferred_element_type=F32)
        ref[...] = jnp.where(same, full, 0.0).astype(BF)

    def local_step(x, c):
        for h in range(2):
            high, low = split(f_in[:, x, h * 8:(h + 1) * 8, :].reshape(384, NZ))
            local = dot(a_high[...], high) + dot(a_low[...], high) + dot(a_high[...], low) + shift[:, :1]
            held[:, x, h * 8:(h + 1) * 8, :] = local.reshape(CH, 8, NZ)
        return c

    lax.fori_loop(0, 8, local_step, 0)

    def along_x(t):
        for pair in range(4):
            data = jnp.concatenate(
                [recv1[t, pl.ds(2 * pair + h, 128, stride=8), :] for h in range(2)], axis=1)
            prod = dot(lx[...], jnp.concatenate(split(data), axis=0))
            prod = prod[:64] + prod[64:]
            for h in range(2):
                piece = prod[:, h * 128:(h + 1) * 128]
                send2[t, pl.ds(2 * pair + h, 32, stride=8), :] = piece[:32] + sign * pltpu.roll(piece[32:], 64, 1)
        send_all(copy2, t, my, H)
        recv2[t, pl.ds(my * 32, 32), :] = send2[t, pl.ds(my * 32, 32), :]

    def along_y(t):
        all2(t).wait_recv()
        data = recv2[t].reshape(H, 4, 8, 128)
        data = jnp.concatenate([data[:, i].reshape(64, 128) for i in range(4)], axis=1)
        prod = dot(ly[...], jnp.concatenate(split(data), axis=0))
        prod = prod[:128] + prod[128:]
        rows = []
        for i in range(4):
            piece = prod[:, i * 128:(i + 1) * 128]
            u = jnp.where(first, piece[:32], piece[64:96])
            w = jnp.where(first, piece[32:64], piece[96:])
            v = u + sign * pltpu.roll(w, 64, 1)
            rows.append(v + pltpu.roll(v, 32, 1))
        v = jnp.concatenate(rows, axis=0)
        v_exp[t] = dot(jnp.concatenate(split(v), axis=1), e_in[1 if t == TB else 0])

    def mix(q):
        t = (TA, TC)[q]

        def body(i, c):
            at = pl.ds(pl.multiple_of(i * 32, 32), 32)
            for part in range(3):
                real = jnp.zeros((32, 128), F32)
                imag = jnp.zeros((32, 128), F32)
                for b in range(6):
                    col = b * 384 + part * 128
                    if b < 4:
                        source, base, gap = t, b * 768 + part * 128, 384
                    else:
                        source, base, gap = TB, (b - 4) * 1536 + q * 384 + part * 128, 768
                    vr = v_exp[source, at, base:base + 128]
                    vi = v_exp[source, at, base + gap:base + gap + 128]
                    w0 = w_in[0, q, i, :, col:col + 128]
                    w1 = w_in[1, q, i, :, col:col + 128]
                    real += vr * w0 - vi * w1
                    imag += vr * w1 + vi * w0
                col = q * 768 + part * 128
                h_acc[at, col:col + 128] = real
                h_acc[at, col + 384:col + 384 + 128] = imag
            return c

        lax.fori_loop(0, 4, body, 0)

    def collect(t):
        if t == TB:
            source, table = h_acc[...], r_in[768:, :]
        else:
            source, table = h_acc[:, (0 if t == TA else 768):(768 if t == TA else 1536)], r_in[:768, :]
        high, low = split(source)
        return dot(high, table) + dot(low, table)

    def back_y(t):
        h_all = collect(t)
        data = jnp.concatenate([h_all[i * 32:(i + 1) * 32] for i in range(4)], axis=1)
        high, low = split(data)
        prod = dot(liy[...], jnp.concatenate([high, low, high], axis=0))
        for i in range(4):
            piece = prod[:, i * 128:(i + 1) * 128]
            a = jnp.where(first, piece[:64], piece[64:128])
            b = jnp.where(first, piece[128:192], piece[192:])
            q = a - sign * pltpu.roll(b, 64, 1)
            send3[t, :, i * 8:(i + 1) * 8, :] = q.reshape(H, 8, 128)
        send_all(copy3, t, my, H)
        recv3[t, pl.ds(my * 32, 32), :] = send3[t, my]

    def back_x(t):
        all3(t).wait_recv()
        for pair in range(4):
            data = jnp.concatenate(
                [recv3[t, pl.ds(2 * pair + h, 32, stride=8), :] for h in range(2)], axis=1)
            high, low = split(data)
            prod = dot(lix[...], jnp.concatenate([high, low, high], axis=0))
            for h in range(2):
                piece = prod[:, h * 128:(h + 1) * 128]
                send4[t, pl.ds(2 * pair + h, 128, stride=8), :] = piece[:128] - sign * pltpu.roll(piece[128:], 64, 1)
        send_all(copy4, t, me, G)
        if t == TB:
            own4().start()
        else:
            recv4[t, me] = send4[t, pl.ds(me * 64, 64), :]

    for copy in const_copies:
        copy.wait()
    all1(TB).wait_recv()
    along_x(TB)
    all1(TA).wait_recv()
    along_x(TA)
    for r in range(2):
        for q in range(2):
            weight_copy(r, q).wait()
    along_y(TB)
    all1(TC).wait_recv()
    along_x(TC)
    along_y(TA)
    mix(0)
    back_y(TA)
    along_y(TC)
    mix(1)
    back_y(TC)
    back_x(TA)
    back_y(TB)
    back_x(TC)
    back_x(TB)

    for t in range(CT):
        all1(t).wait_send()
        all2(t).wait_send()
        all3(t).wait_send()
    all4(TA).wait_recv()

    def turn(x, c):
        at = pl.ds(pl.multiple_of(x * 8, 8), 8)
        for o, tile in enumerate(lanes16([recv4[TA, s, at, :] for s in range(G)], lane)):
            recv4[TA, o, at, :] = tile
        return c

    lax.fori_loop(0, 8, turn, 0)
    all4(TC).wait_recv()

    def finish(xq, c):
        tiles = []
        for x in range(2):
            at = pl.ds(xq * 16 + x * 8, 8)
            odd = lanes16([recv4[TC, s, at, :] for s in range(G)], lane)
            tiles.append([trade(recv4[TA, o, at, :], odd[o], 16, lane) for o in range(16)])
        rows = jnp.concatenate([tiles[x][o][p] for p in range(2) for o in range(16) for x in range(2)], axis=0)
        high, low = split(rows)
        spectral = dot(jnp.concatenate([high, low], axis=1), ez_in[...]) + dot(high, el_in[...])
        for h in range(2):
            at = (pl.ds(0, 32), pl.ds(xq * 2, 2), pl.ds(h * 8, 8), slice(None))
            held[at] = gelu(held[at] + spectral[:, h * NZ:(h + 1) * NZ].reshape(32, 2, 8, NZ))
        return c

    lax.fori_loop(0, 4, finish, 0)
    for t in range(CT):
        all4(t).wait_send()
    own4().wait()
    all4(TB).wait_recv()


def final_kernel(pre, modes, ez, el, out, work, ez_in, el_in, v_sem, o_sem, c_sem):
    lane = lax.broadcasted_iota(jnp.int32, (8, 128), 1)
    done = CH - 16
    small = [pltpu.make_async_copy(ez, ez_in, c_sem.at[0]), pltpu.make_async_copy(el, el_in, c_sem.at[1])]
    store = [pltpu.make_async_copy(work.at[p], out.at[pl.ds(done, 16), pl.ds(2 * p, 2)], v_sem.at[p]) for p in range(4)]
    give = [pltpu.make_async_copy(pre.at[pl.ds(8 * p, 8)], out.at[pl.ds(8 * p, 8)], o_sem.at[p]) for p in range(4)]
    for copy in small + give:
        copy.start()
    for copy in small:
        copy.wait()
    for p in range(4):
        tiles = [lanes16([modes[s, p * 16 + x * 8:p * 16 + (x + 1) * 8, :] for s in range(G)], lane) for x in range(2)]
        high, low = split(jnp.concatenate([tile[o] for o in range(16) for tile in tiles], axis=0))
        spectral = dot(jnp.concatenate([high, low], axis=1), ez_in[...]) + dot(high, el_in[...])
        for h in range(2):
            y = slice(h * 8, (h + 1) * 8)
            part = spectral[:, h * NZ:(h + 1) * NZ].reshape(16, 2, 8, NZ)
            work[p, :, :, y, :] = gelu(pre[done:, 2 * p:2 * p + 2, y, :] + part)
        store[p].start()
    for copy in store + give:
        copy.wait()


def far(array):
    return pltpu.with_memory_space_constraint(array, pltpu.HBM)


def shards(field, spectral_weight, pointwise_weight, channel_bias):
    tz, lx, ly, spread, gather, liy, lix, ez, el = [far(jnp.asarray(c)) for c in constants()]
    field = field.reshape(field.shape[1:])
    scratch = [
        pltpu.VMEM((CH, 8, 16, NZ), F32),
        pltpu.VMEM((2, 2, 4, MODES, CH * CH), F32),
        pltpu.VMEM(spread.shape, BF),
        pltpu.VMEM(gather.shape, BF),
        pltpu.VMEM(ez.shape, BF),
        pltpu.VMEM(el.shape, BF),
        pltpu.VMEM(tz.shape, BF),
        pltpu.VMEM(lx.shape, BF),
        pltpu.VMEM(ly.shape, BF),
        pltpu.VMEM(liy.shape, BF),
        pltpu.VMEM(lix.shape, BF),
        pltpu.VMEM((CH, CH), F32),
        pltpu.VMEM((1, CH), F32),
        pltpu.VMEM((384, 384), BF),
        pltpu.VMEM((384, 384), BF),
        pltpu.VMEM((384, 128), F32),
        pltpu.VMEM((CT, G, 64, 128), F32),
        pltpu.VMEM((CT, G * 64, 128), F32),
        pltpu.VMEM((CT, H * 32, 128), F32),
        pltpu.VMEM((CT, H * 32, 128), F32),
        pltpu.VMEM((CT, H, 32, 128), F32),
        pltpu.VMEM((CT, H * 32, 128), F32),
        pltpu.VMEM((CT, G * 64, 128), F32),
        pltpu.VMEM((2, G, 64, 128), F32),
        pltpu.VMEM((CT, 128, 3072), F32),
        pltpu.VMEM((128, 1536), F32),
    ]
    dma = pltpu.SemaphoreType.DMA
    scratch += [dma((CT,)), dma((2, 2)), dma((11,))]
    scratch += [dma((CT,))] * 8 + [dma]
    pre, last = pl.pallas_call(
        spectral_kernel,
        out_shape=[pltpu.VMEM(field.shape, F32), pltpu.VMEM((G, 64, 128), F32)],
        in_specs=[ANY] * 13,
        out_specs=[VMEM] * 2,
        scratch_shapes=scratch,
        compiler_params=pltpu.CompilerParams(
            collective_id=0, has_side_effects=True, vmem_limit_bytes=46 * 1024 * 1024),
        name="spectral",
    )(far(field), far(spectral_weight), spread, gather, ez, el, far(pointwise_weight), far(channel_bias.reshape(1, CH)),
      tz, lx, ly, liy, lix)
    out = pl.pallas_call(
        final_kernel,
        out_shape=jax.ShapeDtypeStruct(field.shape, F32),
        in_specs=[VMEM, VMEM, ANY, ANY],
        out_specs=ANY,
        scratch_shapes=[
            pltpu.VMEM((4, 16, 2, 16, NZ), F32),
            pltpu.VMEM(ez.shape, BF),
            pltpu.VMEM(el.shape, BF),
            dma((4,)), dma((4,)), dma((2,)),
        ],
        compiler_params=pltpu.CompilerParams(vmem_limit_bytes=40 * 1024 * 1024),
        name="physical",
    )(pre, last, ez, el)
    return out.reshape((1,) + out.shape)


def solution(mesh):
    in_specs = (P(None, None, "px", "py", None), P(None, "py", None, "px", None), P(), P())
    out_specs = P(None, None, "px", "py", None)
    return jax.shard_map(shards, mesh=mesh, in_specs=in_specs, out_specs=out_specs, check_vma=False)
```

```python
import functools
import math

import jax
import jax.numpy as jnp
import ml_dtypes
import numpy as np
from jax import lax
from jax.experimental import pallas as pl
from jax.experimental.pallas import tpu as pltpu
from jax.sharding import PartitionSpec as P

MESH = pl.DeviceIdType.MESH
BF = jnp.bfloat16
F32 = jnp.float32
ANY = pl.BlockSpec(memory_space=pl.ANY)
VMEM = pl.BlockSpec(memory_space=pltpu.VMEM)

NX, NY, NZ, MODES, CH, G, H = 128, 128, 256, 32, 48, 16, 8
CT = CH // 16
TA, TC, TB = range(3)


def halves(table):
    high = table.astype(ml_dtypes.bfloat16)
    low = (table - high.astype(np.float64)).astype(ml_dtypes.bfloat16)
    return high, low


def signed(modes):
    number = np.arange(modes)
    return np.where(number < modes // 2, number, number - modes)


def angles(position, mode, length):
    return 2.0 * math.pi * ((position[:, None] * mode[None, :]) % length) / length


def lane_parts():
    lane = np.arange(128)
    return lane // 64, (lane // 32) % 2, (lane // 16) % 2, lane % 16


@functools.cache
def constants():
    ri, y2, k2, low = lane_parts()
    k = 2 * low + k2
    a = angles(np.arange(NZ), k, NZ)
    wave = np.where(ri[None, :] == 0, np.cos(a), -np.sin(a))
    forward = np.concatenate([wave * (y2 == 0), wave * (y2 == 1)], axis=0)
    tz = np.concatenate(halves(forward), axis=1)
    gain = np.where(k == 0, 1.0, 2.0) / (NX * NY * NZ)
    eh, el = halves((forward * gain).T)
    ez = np.concatenate([eh, eh], axis=0)
    f = signed(MODES)
    ax = angles(np.arange(NX), f, NX)
    ch, cl = halves(np.concatenate([np.cos(ax).T, np.sin(ax).T], axis=0))
    lx = np.concatenate(
        [np.concatenate([ch, ch], axis=1), np.concatenate([cl, np.zeros_like(cl)], axis=1)], axis=0
    )
    ch, cl = halves(np.concatenate([np.cos(ax), np.sin(ax)], axis=0))
    lix = np.concatenate([ch, ch, cl], axis=1)
    y = np.arange(NY).reshape(H, 2, 8)
    parts = [y[:, h].reshape(-1) for h in range(2)]
    ay = [angles(p, f, NY) for p in parts]
    rows = np.concatenate([t for q in ay for t in (np.cos(q).T, np.sin(q).T)], axis=0)
    ch, cl = halves(rows)
    ly = np.concatenate(
        [np.concatenate([ch, ch], axis=1), np.concatenate([cl, np.zeros_like(cl)], axis=1)], axis=0
    )
    rows = np.concatenate([np.cos(ay[0]), np.cos(ay[1]), np.sin(ay[0]), np.sin(ay[1])], axis=0)
    ch, cl = halves(rows)
    liy = np.concatenate([ch, ch, cl], axis=1)
    pair = np.zeros((128, 4, 2, 8, CH))
    both = np.zeros((128, 2, 2, 2, 8, CH))
    for r in range(2):
        for c in range(32):
            pair[r * 64 + 32 + c, c // 8, r, c % 8, :] = 1.0
        for q in range(2):
            for c in range(16):
                both[r * 64 + 32 + q * 16 + c, c // 8, r, q, c % 8, :] = 1.0
    spread = np.stack([pair.reshape(128, -1), both.reshape(128, -1)])
    spread = np.concatenate([spread, spread], axis=1).astype(ml_dtypes.bfloat16)
    pair = np.zeros((2, 8, CH, 128))
    both = np.zeros((2, 2, 8, CH, 128))
    for r in range(2):
        for h in range(2):
            for o in range(32):
                pair[r, :, o, r * 64 + h * 32 + o] = 1.0
            for q in range(2):
                for o in range(16):
                    both[q, r, :, 32 + o, r * 64 + h * 32 + q * 16 + o] = 1.0
    gather = np.concatenate([pair.reshape(-1, 128), both.reshape(-1, 128)], axis=0).astype(ml_dtypes.bfloat16)
    return tz, lx, ly, spread, gather, liy, lix, ez, el


def split(value):
    high = value.astype(BF)
    return high, (value - high.astype(F32)).astype(BF)


def dot(a, b):
    return jnp.dot(a, b, preferred_element_type=F32)


def trade(a, b, step, lane):
    keep = (lane & step) == 0
    return jnp.where(keep, a, pltpu.roll(b, step, 1)), jnp.where(keep, pltpu.roll(a, 128 - step, 1), b)


def lanes16(tiles, lane):
    tiles = [pltpu.roll(tile, c, 1) if c else tile for c, tile in enumerate(tiles)]
    for bit in range(4):
        step = 1 << bit
        shift = (lane & step) != 0
        tiles = [jnp.where(shift, tiles[(h + step) % 16], tiles[h]) for h in range(16)]
    return [pltpu.roll(tiles[16 - g], 128 - g, 1) if g else tiles[0] for g in range(16)]


def gelu(v):
    return 0.5 * v * (1.0 + lax.erf(v * math.sqrt(0.5)))


def spectral_kernel(
    field, weight, spread, gather, ez, el, point_far, bias_far, tz_far, lx_far, ly_far, liy_far, lix_far, held, last,
    f_in, w_in, e_in, r_in, ez_in, el_in, tz, lx, ly, liy, lix, point, bias, a_high, a_low, shift,
    send1, recv1, send2, recv2, send3, recv3, send4, recv4, v_exp, h_acc,
    f_sem, w_sem, c_sem, s1, r1, s2, r2, s3, r3, s4, r4, o_sem,
):
    me, my = lax.axis_index("px"), lax.axis_index("py")

    def field_copy(t):
        return pltpu.make_async_copy(field.at[pl.ds(t * 16, 16)], f_in.at[pl.ds(t * 16, 16)], f_sem.at[t])

    def field_part(half):
        at = (pl.ds(32, 16), pl.ds(half * 4, 4))
        return pltpu.make_async_copy(field.at[at], f_in.at[at], f_sem.at[2 + half])

    def weight_copy(r, q):
        return pltpu.make_async_copy(weight.at[r, :, :, q, :], w_in.at[r, q], w_sem.at[r, q])

    const_copies = [
        pltpu.make_async_copy(spread, e_in, c_sem.at[0]),
        pltpu.make_async_copy(gather, r_in, c_sem.at[1]),
        pltpu.make_async_copy(ez, ez_in, c_sem.at[2]),
        pltpu.make_async_copy(el, el_in, c_sem.at[3]),
        pltpu.make_async_copy(lx_far, lx, c_sem.at[4]),
        pltpu.make_async_copy(ly_far, ly, c_sem.at[5]),
        pltpu.make_async_copy(liy_far, liy, c_sem.at[6]),
        pltpu.make_async_copy(lix_far, lix, c_sem.at[7]),
    ]
    conv_copies = [
        pltpu.make_async_copy(point_far, point, c_sem.at[9]),
        pltpu.make_async_copy(bias_far, bias, c_sem.at[10]),
    ]
    first_table = pltpu.make_async_copy(tz_far, tz, c_sem.at[8])
    first_table.start()
    for half in range(2):
        field_part(half).start()
    for t in range(2):
        field_copy(t).start()

    barrier = pltpu.get_barrier_semaphore()

    def greet_x(d, c):
        pl.semaphore_signal(barrier, inc=1, device_id=(lax.rem(me + d, G), my), device_id_type=MESH)
        return c

    def greet_y(d, c):
        pl.semaphore_signal(barrier, inc=1, device_id=(me, lax.rem(my + d, H)), device_id_type=MESH)
        return c

    lax.fori_loop(1, G, greet_x, 0)
    lax.fori_loop(1, H, greet_y, 0)

    def copy1(t, first_row, rows, target, source):
        return pltpu.make_async_remote_copy(
            send1.at[t, target, pl.ds(first_row, rows)], recv1.at[t, pl.ds(source * 64 + first_row, rows)],
            s1.at[t], r1.at[t], device_id=(target, my), device_id_type=MESH)

    def send1_all(t, first_row, rows):
        def body(d, c):
            copy1(t, first_row, rows, lax.rem(me + d, G), me).start()
            return c
        lax.fori_loop(1, G, body, 0)

    def copy2(t, target, source):
        return pltpu.make_async_remote_copy(
            send2.at[t, pl.ds(target * 32, 32)], recv2.at[t, pl.ds(source * 32, 32)], s2.at[t],
            r2.at[t], device_id=(me, target), device_id_type=MESH)

    def copy3(t, target, source):
        return pltpu.make_async_remote_copy(
            send3.at[t, target], recv3.at[t, pl.ds(source * 32, 32)], s3.at[t], r3.at[t],
            device_id=(me, target), device_id_type=MESH)

    def landing(t):
        return last if t == TB else recv4.at[t]

    def copy4(t, target, source):
        return pltpu.make_async_remote_copy(
            send4.at[t, pl.ds(target * 64, 64)], landing(t).at[source], s4.at[t], r4.at[t],
            device_id=(target, my), device_id_type=MESH)

    def own4():
        return pltpu.make_async_copy(send4.at[TB, pl.ds(me * 64, 64)], last.at[me], o_sem)

    def send_all(copy, t, index, count):
        def body(d, c):
            copy(t, lax.rem(index + d, count), index).start()
            return c
        lax.fori_loop(1, count, body, 0)

    def all1(t):
        return pltpu.make_async_remote_copy(
            send1.at[t, pl.ds(0, G - 1)], recv1.at[t, pl.ds(0, (G - 1) * 64)], s1.at[t], r1.at[t],
            device_id=(lax.rem(me + 1, G), my), device_id_type=MESH)

    def all2(t):
        return pltpu.make_async_remote_copy(
            send2.at[t, pl.ds(0, (H - 1) * 32)], recv2.at[t, pl.ds(0, (H - 1) * 32)], s2.at[t], r2.at[t],
            device_id=(me, lax.rem(my + 1, H)), device_id_type=MESH)

    def all3(t):
        return pltpu.make_async_remote_copy(
            send3.at[t, pl.ds(0, H - 1)], recv3.at[t, pl.ds(0, (H - 1) * 32)], s3.at[t], r3.at[t],
            device_id=(me, lax.rem(my + 1, H)), device_id_type=MESH)

    def all4(t):
        return pltpu.make_async_remote_copy(
            send4.at[t, pl.ds(0, (G - 1) * 64)], landing(t).at[pl.ds(0, G - 1)], s4.at[t], r4.at[t],
            device_id=(lax.rem(me + 1, G), my), device_id_type=MESH)

    lane = lax.broadcasted_iota(jnp.int32, (8, 128), 1)
    wide = lax.broadcasted_iota(jnp.int32, (1, 128), 1)
    sign = jnp.where(wide < 64, 1.0, -1.0).astype(F32)
    first = (wide & 32) == 0

    def z_tiles(first_c, count, x, xs):
        block = f_in[first_c:first_c + count, pl.ds(x, xs)]
        rows = jnp.concatenate(
            [block[:, :, :8].reshape(count * xs * 8, NZ), block[:, :, 8:].reshape(count * xs * 8, NZ)], axis=1)
        high, low = split(rows)
        prod = dot(high, tz[...])
        z = (prod[:, :128] + prod[:, 128:] + dot(low, tz[:, :128])).reshape(count, xs, 8, 128)
        return [[lanes16([z[g * 16 + c, q] for c in range(16)], lane) for g in range(count // 16)] for q in range(xs)]

    def z_both(xq, c):
        for q, (tiles,) in enumerate(z_tiles(32, 16, xq * 4, 4)):
            for g in range(G):
                send1[TB, g, pl.ds(xq * 32 + q * 8, 8), :] = tiles[g]
        return c

    def z_pair(xq, c):
        for q, (even, odd) in enumerate(z_tiles(0, 32, xq * 2, 2)):
            for g in range(G):
                a, b = trade(even[g], odd[g], 16, lane)
                send1[TA, g, pl.ds(xq * 16 + q * 8, 8), :] = a
                send1[TC, g, pl.ds(xq * 16 + q * 8, 8), :] = b
        return c

    first_table.wait()
    field_part(0).wait()
    z_both(0, 0)
    pl.semaphore_wait(barrier, G + H - 2)
    send1_all(TB, 0, 32)
    for copy in conv_copies:
        copy.start()
    field_part(1).wait()
    z_both(1, 0)
    send1_all(TB, 32, 32)
    field_copy(0).wait()
    field_copy(1).wait()
    for half in range(2):
        lax.fori_loop(half * 2, half * 2 + 2, z_pair, 0)
    send1_all(TA, 0, 64)
    send1_all(TC, 0, 64)
    for t in range(CT):
        recv1[t, pl.ds(me * 64, 64), :] = send1[t, me]

    for copy in const_copies:
        copy.start()
    for r in range(2):
        for q in range(2):
            weight_copy(r, q).start()

    for copy in conv_copies:
        copy.wait()
    row = lax.broadcasted_iota(jnp.int32, (384, CH), 0)
    col = lax.broadcasted_iota(jnp.int32, (384, CH), 1)
    pick = row // 8 == col
    shift[...] = jnp.sum(jnp.where(pick, bias[...], 0.0), axis=1, keepdims=True) + jnp.zeros((384, 128), F32)
    picked = pick.astype(F32).astype(BF)
    row = lax.broadcasted_iota(jnp.int32, (384, 384), 0)
    col = lax.broadcasted_iota(jnp.int32, (384, 384), 1)
    same = (row % 8) == (col % 8)
    for piece, ref in zip(split(point[...]), (a_high, a_low)):
        tall = lax.dot_general(picked, piece, (((1,), (1,)), ((), ())), preferred_element_type=F32)
        full = lax.dot_general(tall.astype(BF), picked, (((1,), (1,)), ((), ())), preferred_element_type=F32)
        ref[...] = jnp.where(same, full, 0.0).astype(BF)

    def local_step(x, c):
        for h in range(2):
            high, low = split(f_in[:, x, h * 8:(h + 1) * 8, :].reshape(384, NZ))
            local = dot(a_high[...], high) + dot(a_low[...], high) + dot(a_high[...], low) + shift[:, :1]
            held[:, x, h * 8:(h + 1) * 8, :] = local.reshape(CH, 8, NZ)
        return c

    lax.fori_loop(0, 8, local_step, 0)

    def along_x(t):
        for pair in range(4):
            data = jnp.concatenate(
                [recv1[t, pl.ds(2 * pair + h, 128, stride=8), :] for h in range(2)], axis=1)
            prod = dot(lx[...], jnp.concatenate(split(data), axis=0))
            prod = prod[:64] + prod[64:]
            for h in range(2):
                piece = prod[:, h * 128:(h + 1) * 128]
                send2[t, pl.ds(2 * pair + h, 32, stride=8), :] = piece[:32] + sign * pltpu.roll(piece[32:], 64, 1)
        send_all(copy2, t, my, H)
        recv2[t, pl.ds(my * 32, 32), :] = send2[t, pl.ds(my * 32, 32), :]

    def along_y(t):
        all2(t).wait_recv()
        data = recv2[t].reshape(H, 4, 8, 128)
        data = jnp.concatenate([data[:, i].reshape(64, 128) for i in range(4)], axis=1)
        prod = dot(ly[...], jnp.concatenate(split(data), axis=0))
        prod = prod[:128] + prod[128:]
        rows = []
        for i in range(4):
            piece = prod[:, i * 128:(i + 1) * 128]
            u = jnp.where(first, piece[:32], piece[64:96])
            w = jnp.where(first, piece[32:64], piece[96:])
            v = u + sign * pltpu.roll(w, 64, 1)
            rows.append(v + pltpu.roll(v, 32, 1))
        v = jnp.concatenate(rows, axis=0)
        v_exp[t] = dot(jnp.concatenate(split(v), axis=1), e_in[1 if t == TB else 0])

    def mix(q):
        t = (TA, TC)[q]

        def body(i, c):
            at = pl.ds(pl.multiple_of(i * 32, 32), 32)
            for part in range(3):
                real = jnp.zeros((32, 128), F32)
                imag = jnp.zeros((32, 128), F32)
                for b in range(6):
                    col = b * 384 + part * 128
                    if b < 4:
                        source, base, gap = t, b * 768 + part * 128, 384
                    else:
                        source, base, gap = TB, (b - 4) * 1536 + q * 384 + part * 128, 768
                    vr = v_exp[source, at, base:base + 128]
                    vi = v_exp[source, at, base + gap:base + gap + 128]
                    w0 = w_in[0, q, i, :, col:col + 128]
                    w1 = w_in[1, q, i, :, col:col + 128]
                    real += vr * w0 - vi * w1
                    imag += vr * w1 + vi * w0
                col = q * 768 + part * 128
                h_acc[at, col:col + 128] = real
                h_acc[at, col + 384:col + 384 + 128] = imag
            return c

        lax.fori_loop(0, 4, body, 0)

    def collect(t):
        if t == TB:
            source, table = h_acc[...], r_in[768:, :]
        else:
            source, table = h_acc[:, (0 if t == TA else 768):(768 if t == TA else 1536)], r_in[:768, :]
        both = dot(jnp.concatenate(split(source), axis=0), table)
        return both[:128] + both[128:]

    def back_y(t):
        h_all = collect(t)
        data = jnp.concatenate([h_all[i * 32:(i + 1) * 32] for i in range(4)], axis=1)
        high, low = split(data)
        prod = dot(liy[...], jnp.concatenate([high, low, high], axis=0))
        for i in range(4):
            piece = prod[:, i * 128:(i + 1) * 128]
            a = jnp.where(first, piece[:64], piece[64:128])
            b = jnp.where(first, piece[128:192], piece[192:])
            q = a - sign * pltpu.roll(b, 64, 1)
            send3[t, :, i * 8:(i + 1) * 8, :] = q.reshape(H, 8, 128)
        send_all(copy3, t, my, H)
        recv3[t, pl.ds(my * 32, 32), :] = send3[t, my]

    def back_x(t):
        all3(t).wait_recv()
        for pair in range(4):
            data = jnp.concatenate(
                [recv3[t, pl.ds(2 * pair + h, 32, stride=8), :] for h in range(2)], axis=1)
            high, low = split(data)
            prod = dot(lix[...], jnp.concatenate([high, low, high], axis=0))
            for h in range(2):
                piece = prod[:, h * 128:(h + 1) * 128]
                send4[t, pl.ds(2 * pair + h, 128, stride=8), :] = piece[:128] - sign * pltpu.roll(piece[128:], 64, 1)
        send_all(copy4, t, me, G)
        if t == TB:
            own4().start()
        else:
            recv4[t, me] = send4[t, pl.ds(me * 64, 64), :]

    for copy in const_copies:
        copy.wait()
    all1(TB).wait_recv()
    along_x(TB)
    all1(TA).wait_recv()
    along_x(TA)
    for r in range(2):
        for q in range(2):
            weight_copy(r, q).wait()
    along_y(TB)
    all1(TC).wait_recv()
    along_x(TC)
    along_y(TA)
    mix(0)
    back_y(TA)
    along_y(TC)
    mix(1)
    back_y(TC)
    back_x(TA)
    back_y(TB)
    back_x(TC)
    back_x(TB)

    for t in range(CT):
        all1(t).wait_send()
        all2(t).wait_send()
        all3(t).wait_send()
    all4(TA).wait_recv()

    def turn(x, c):
        at = pl.ds(pl.multiple_of(x * 8, 8), 8)
        for o, tile in enumerate(lanes16([recv4[TA, s, at, :] for s in range(G)], lane)):
            recv4[TA, o, at, :] = tile
        return c

    lax.fori_loop(0, 8, turn, 0)
    all4(TC).wait_recv()

    def finish(xq, c):
        tiles = []
        for x in range(2):
            at = pl.ds(xq * 16 + x * 8, 8)
            odd = lanes16([recv4[TC, s, at, :] for s in range(G)], lane)
            tiles.append([trade(recv4[TA, o, at, :], odd[o], 16, lane) for o in range(16)])
        rows = jnp.concatenate([tiles[x][o][p] for p in range(2) for o in range(16) for x in range(2)], axis=0)
        high, low = split(rows)
        spectral = dot(jnp.concatenate([high, low], axis=1), ez_in[...]) + dot(high, el_in[...])
        for h in range(2):
            at = (pl.ds(0, 32), pl.ds(xq * 2, 2), pl.ds(h * 8, 8), slice(None))
            held[at] = gelu(held[at] + spectral[:, h * NZ:(h + 1) * NZ].reshape(32, 2, 8, NZ))
        return c

    lax.fori_loop(0, 4, finish, 0)
    for t in range(CT):
        all4(t).wait_send()
    own4().wait()
    all4(TB).wait_recv()


def final_kernel(pre, modes, ez, el, out, work, ez_in, el_in, v_sem, o_sem, c_sem):
    lane = lax.broadcasted_iota(jnp.int32, (8, 128), 1)
    done = CH - 16
    small = [pltpu.make_async_copy(ez, ez_in, c_sem.at[0]), pltpu.make_async_copy(el, el_in, c_sem.at[1])]
    store = [pltpu.make_async_copy(work.at[p], out.at[pl.ds(done, 16), pl.ds(2 * p, 2)], v_sem.at[p]) for p in range(4)]
    give = [pltpu.make_async_copy(pre.at[pl.ds(8 * p, 8)], out.at[pl.ds(8 * p, 8)], o_sem.at[p]) for p in range(4)]
    for copy in small + give:
        copy.start()
    for p in range(4):
        tiles = [lanes16([modes[s, p * 16 + x * 8:p * 16 + (x + 1) * 8, :] for s in range(G)], lane) for x in range(2)]
        high, low = split(jnp.concatenate([tile[o] for o in range(16) for tile in tiles], axis=0))
        if p == 0:
            for copy in small:
                copy.wait()
        spectral = dot(jnp.concatenate([high, low], axis=1), ez_in[...]) + dot(high, el_in[...])
        for h in range(2):
            y = slice(h * 8, (h + 1) * 8)
            part = spectral[:, h * NZ:(h + 1) * NZ].reshape(16, 2, 8, NZ)
            work[p, :, :, y, :] = gelu(pre[done:, 2 * p:2 * p + 2, y, :] + part)
        store[p].start()
    for copy in store + give:
        copy.wait()


def far(array):
    return pltpu.with_memory_space_constraint(array, pltpu.HBM)


def shards(field, spectral_weight, pointwise_weight, channel_bias):
    tz, lx, ly, spread, gather, liy, lix, ez, el = [far(jnp.asarray(c)) for c in constants()]
    field = field.reshape(field.shape[1:])
    scratch = [
        pltpu.VMEM((CH, 8, 16, NZ), F32),
        pltpu.VMEM((2, 2, 4, MODES, CH * CH), F32),
        pltpu.VMEM(spread.shape, BF),
        pltpu.VMEM(gather.shape, BF),
        pltpu.VMEM(ez.shape, BF),
        pltpu.VMEM(el.shape, BF),
        pltpu.VMEM(tz.shape, BF),
        pltpu.VMEM(lx.shape, BF),
        pltpu.VMEM(ly.shape, BF),
        pltpu.VMEM(liy.shape, BF),
        pltpu.VMEM(lix.shape, BF),
        pltpu.VMEM((CH, CH), F32),
        pltpu.VMEM((1, CH), F32),
        pltpu.VMEM((384, 384), BF),
        pltpu.VMEM((384, 384), BF),
        pltpu.VMEM((384, 128), F32),
        pltpu.VMEM((CT, G, 64, 128), F32),
        pltpu.VMEM((CT, G * 64 + 8, 128), F32),
        pltpu.VMEM((CT, H * 32 + 8, 128), F32),
        pltpu.VMEM((CT, H * 32, 128), F32),
        pltpu.VMEM((CT, H, 32, 128), F32),
        pltpu.VMEM((CT, H * 32 + 8, 128), F32),
        pltpu.VMEM((CT, G * 64 + 8, 128), F32),
        pltpu.VMEM((2, G, 64, 128), F32),
        pltpu.VMEM((CT, 128, 3072), F32),
        pltpu.VMEM((128, 1536), F32),
    ]
    dma = pltpu.SemaphoreType.DMA
    scratch += [dma((4,)), dma((2, 2)), dma((11,))]
    scratch += [dma((CT,))] * 8 + [dma]
    pre, last = pl.pallas_call(
        spectral_kernel,
        out_shape=[pltpu.VMEM(field.shape, F32), pltpu.VMEM((G, 64, 128), F32)],
        in_specs=[ANY] * 13,
        out_specs=[VMEM] * 2,
        scratch_shapes=scratch,
        compiler_params=pltpu.CompilerParams(
            collective_id=0, has_side_effects=True, vmem_limit_bytes=46 * 1024 * 1024),
        name="spectral",
    )(far(field), far(spectral_weight), spread, gather, ez, el, far(pointwise_weight), far(channel_bias.reshape(1, CH)),
      tz, lx, ly, liy, lix)
    out = pl.pallas_call(
        final_kernel,
        out_shape=jax.ShapeDtypeStruct(field.shape, F32),
        in_specs=[VMEM, VMEM, ANY, ANY],
        out_specs=ANY,
        scratch_shapes=[
            pltpu.VMEM((4, 16, 2, 16, NZ), F32),
            pltpu.VMEM(ez.shape, BF),
            pltpu.VMEM(el.shape, BF),
            dma((4,)), dma((4,)), dma((2,)),
        ],
        compiler_params=pltpu.CompilerParams(vmem_limit_bytes=40 * 1024 * 1024),
        name="physical",
    )(pre, last, ez, el)
    return out.reshape((1,) + out.shape)


def solution(mesh):
    in_specs = (P(None, None, "px", "py", None), P(None, "py", None, "px", None), P(), P())
    out_specs = P(None, None, "px", "py", None)
    return jax.shard_map(shards, mesh=mesh, in_specs=in_specs, out_specs=out_specs, check_vma=False)
```

```python
import functools
import math

import jax
import jax.numpy as jnp
import ml_dtypes
import numpy as np
from jax import lax
from jax.experimental import pallas as pl
from jax.experimental.pallas import tpu as pltpu
from jax.sharding import PartitionSpec as P

MESH = pl.DeviceIdType.MESH
BF = jnp.bfloat16
F32 = jnp.float32
ANY = pl.BlockSpec(memory_space=pl.ANY)
VMEM = pl.BlockSpec(memory_space=pltpu.VMEM)

NX, NY, NZ, MODES, CH, G, H = 128, 128, 256, 32, 48, 16, 8
CT = CH // 16
TA, TC, TB = range(3)


def halves(table):
    high = table.astype(ml_dtypes.bfloat16)
    low = (table - high.astype(np.float64)).astype(ml_dtypes.bfloat16)
    return high, low


def signed(modes):
    number = np.arange(modes)
    return np.where(number < modes // 2, number, number - modes)


def angles(position, mode, length):
    return 2.0 * math.pi * ((position[:, None] * mode[None, :]) % length) / length


def lane_parts():
    lane = np.arange(128)
    return lane // 64, (lane // 32) % 2, (lane // 16) % 2, lane % 16


@functools.cache
def constants():
    ri, y2, k2, low = lane_parts()
    k = 2 * low + k2
    a = angles(np.arange(NZ), k, NZ)
    wave = np.where(ri[None, :] == 0, np.cos(a), -np.sin(a))
    forward = np.concatenate([wave * (y2 == 0), wave * (y2 == 1)], axis=0)
    tz = np.concatenate(halves(forward), axis=1)
    gain = np.where(k == 0, 1.0, 2.0) / (NX * NY * NZ)
    eh, el = halves((forward * gain).T)
    ez = np.concatenate([eh, eh], axis=0)
    f = signed(MODES)
    ax = angles(np.arange(NX), f, NX)
    ch, cl = halves(np.concatenate([np.cos(ax).T, np.sin(ax).T], axis=0))
    lx = np.concatenate(
        [np.concatenate([ch, ch], axis=1), np.concatenate([cl, np.zeros_like(cl)], axis=1)], axis=0
    )
    ch, cl = halves(np.concatenate([np.cos(ax), np.sin(ax)], axis=0))
    lix = np.concatenate([ch, ch, cl], axis=1)
    y = np.arange(NY).reshape(H, 2, 8)
    parts = [y[:, h].reshape(-1) for h in range(2)]
    ay = [angles(p, f, NY) for p in parts]
    rows = np.concatenate([t for q in ay for t in (np.cos(q).T, np.sin(q).T)], axis=0)
    ch, cl = halves(rows)
    ly = np.concatenate(
        [np.concatenate([ch, ch], axis=1), np.concatenate([cl, np.zeros_like(cl)], axis=1)], axis=0
    )
    rows = np.concatenate([np.cos(ay[0]), np.cos(ay[1]), np.sin(ay[0]), np.sin(ay[1])], axis=0)
    ch, cl = halves(rows)
    liy = np.concatenate([ch, ch, cl], axis=1)
    pair = np.zeros((128, 4, 2, 8, CH))
    both = np.zeros((128, 2, 2, 2, 8, CH))
    for r in range(2):
        for c in range(32):
            pair[r * 64 + 32 + c, c // 8, r, c % 8, :] = 1.0
        for q in range(2):
            for c in range(16):
                both[r * 64 + 32 + q * 16 + c, c // 8, r, q, c % 8, :] = 1.0
    spread = np.stack([pair.reshape(128, -1), both.reshape(128, -1)])
    spread = np.concatenate([spread, spread], axis=1).astype(ml_dtypes.bfloat16)
    pair = np.zeros((2, 8, CH, 128))
    both = np.zeros((2, 2, 8, CH, 128))
    for r in range(2):
        for h in range(2):
            for o in range(32):
                pair[r, :, o, r * 64 + h * 32 + o] = 1.0
            for q in range(2):
                for o in range(16):
                    both[q, r, :, 32 + o, r * 64 + h * 32 + q * 16 + o] = 1.0
    gather = np.concatenate([pair.reshape(-1, 128), both.reshape(-1, 128)], axis=0).astype(ml_dtypes.bfloat16)
    return tz, lx, ly, spread, gather, liy, lix, ez, el


def split(value):
    high = value.astype(BF)
    return high, (value - high.astype(F32)).astype(BF)


def dot(a, b):
    return jnp.dot(a, b, preferred_element_type=F32)


def trade(a, b, step, lane):
    keep = (lane & step) == 0
    return jnp.where(keep, a, pltpu.roll(b, step, 1)), jnp.where(keep, pltpu.roll(a, 128 - step, 1), b)


def lanes16(tiles, lane):
    tiles = [pltpu.roll(tile, c, 1) if c else tile for c, tile in enumerate(tiles)]
    for bit in range(4):
        step = 1 << bit
        shift = (lane & step) != 0
        tiles = [jnp.where(shift, tiles[(h + step) % 16], tiles[h]) for h in range(16)]
    return [pltpu.roll(tiles[16 - g], 128 - g, 1) if g else tiles[0] for g in range(16)]


def gelu(v):
    return 0.5 * v * (1.0 + lax.erf(v * math.sqrt(0.5)))


def spectral_kernel(
    field, weight, spread, gather, ez, el, point_far, bias_far, tz_far, lx_far, ly_far, liy_far, lix_far, held, last,
    f_in, w_in, e_in, r_in, ez_in, el_in, tz, lx, ly, liy, lix, point, bias, a_high, a_low, shift,
    send1, recv1, send2, recv2, send3, recv3, send4, recv4, v_exp, h_acc,
    f_sem, w_sem, c_sem, s1, r1, s2, r2, s3, r3, s4, r4, o_sem,
):
    me, my = lax.axis_index("px"), lax.axis_index("py")

    def field_copy(t):
        return pltpu.make_async_copy(field.at[pl.ds(t * 16, 16)], f_in.at[pl.ds(t * 16, 16)], f_sem.at[t])

    def field_part(half):
        at = (pl.ds(32, 16), pl.ds(half * 4, 4))
        return pltpu.make_async_copy(field.at[at], f_in.at[at], f_sem.at[2 + half])

    def weight_copy(r, q):
        return pltpu.make_async_copy(weight.at[r, :, :, q, :], w_in.at[r, q], w_sem.at[r, q])

    const_copies = [
        pltpu.make_async_copy(spread, e_in, c_sem.at[0]),
        pltpu.make_async_copy(gather, r_in, c_sem.at[1]),
        pltpu.make_async_copy(ez, ez_in, c_sem.at[2]),
        pltpu.make_async_copy(el, el_in, c_sem.at[3]),
        pltpu.make_async_copy(lx_far, lx, c_sem.at[4]),
        pltpu.make_async_copy(ly_far, ly, c_sem.at[5]),
        pltpu.make_async_copy(liy_far, liy, c_sem.at[6]),
        pltpu.make_async_copy(lix_far, lix, c_sem.at[7]),
    ]
    conv_copies = [
        pltpu.make_async_copy(point_far, point, c_sem.at[9]),
        pltpu.make_async_copy(bias_far, bias, c_sem.at[10]),
    ]
    first_table = pltpu.make_async_copy(tz_far, tz, c_sem.at[8])
    first_table.start()
    for half in range(2):
        field_part(half).start()
    for t in range(2):
        field_copy(t).start()

    barrier = pltpu.get_barrier_semaphore()

    def greet_x(d, c):
        pl.semaphore_signal(barrier, inc=1, device_id=(lax.rem(me + d, G), my), device_id_type=MESH)
        return c

    def greet_y(d, c):
        pl.semaphore_signal(barrier, inc=1, device_id=(me, lax.rem(my + d, H)), device_id_type=MESH)
        return c

    lax.fori_loop(1, G, greet_x, 0)
    lax.fori_loop(1, H, greet_y, 0)

    def copy1(t, first_row, rows, target, source):
        return pltpu.make_async_remote_copy(
            send1.at[t, target, pl.ds(first_row, rows)], recv1.at[t, pl.ds(source * 64 + first_row, rows)],
            s1.at[t], r1.at[t], device_id=(target, my), device_id_type=MESH)

    def send1_all(t, first_row, rows):
        def body(d, c):
            copy1(t, first_row, rows, lax.rem(me + d, G), me).start()
            return c
        lax.fori_loop(1, G, body, 0, unroll=True)

    def copy2(t, target, source):
        return pltpu.make_async_remote_copy(
            send2.at[t, pl.ds(target * 32, 32)], recv2.at[t, pl.ds(source * 32, 32)], s2.at[t],
            r2.at[t], device_id=(me, target), device_id_type=MESH)

    def copy3(t, target, source):
        return pltpu.make_async_remote_copy(
            send3.at[t, target], recv3.at[t, pl.ds(source * 32, 32)], s3.at[t], r3.at[t],
            device_id=(me, target), device_id_type=MESH)

    def landing(t):
        return last if t == TB else recv4.at[t]

    def copy4(t, target, source):
        return pltpu.make_async_remote_copy(
            send4.at[t, pl.ds(target * 64, 64)], landing(t).at[source], s4.at[t], r4.at[t],
            device_id=(target, my), device_id_type=MESH)

    def own4():
        return pltpu.make_async_copy(send4.at[TB, pl.ds(me * 64, 64)], last.at[me], o_sem)

    def send_all(copy, t, index, count):
        def body(d, c):
            copy(t, lax.rem(index + d, count), index).start()
            return c
        lax.fori_loop(1, count, body, 0, unroll=True)

    def all1(t):
        return pltpu.make_async_remote_copy(
            send1.at[t, pl.ds(0, G - 1)], recv1.at[t, pl.ds(0, (G - 1) * 64)], s1.at[t], r1.at[t],
            device_id=(lax.rem(me + 1, G), my), device_id_type=MESH)

    def all2(t):
        return pltpu.make_async_remote_copy(
            send2.at[t, pl.ds(0, (H - 1) * 32)], recv2.at[t, pl.ds(0, (H - 1) * 32)], s2.at[t], r2.at[t],
            device_id=(me, lax.rem(my + 1, H)), device_id_type=MESH)

    def all3(t):
        return pltpu.make_async_remote_copy(
            send3.at[t, pl.ds(0, H - 1)], recv3.at[t, pl.ds(0, (H - 1) * 32)], s3.at[t], r3.at[t],
            device_id=(me, lax.rem(my + 1, H)), device_id_type=MESH)

    def all4(t):
        return pltpu.make_async_remote_copy(
            send4.at[t, pl.ds(0, (G - 1) * 64)], landing(t).at[pl.ds(0, G - 1)], s4.at[t], r4.at[t],
            device_id=(lax.rem(me + 1, G), my), device_id_type=MESH)

    lane = lax.broadcasted_iota(jnp.int32, (8, 128), 1)
    wide = lax.broadcasted_iota(jnp.int32, (1, 128), 1)
    sign = jnp.where(wide < 64, 1.0, -1.0).astype(F32)
    first = (wide & 32) == 0

    def z_tiles(first_c, count, x, xs):
        block = f_in[first_c:first_c + count, pl.ds(x, xs)]
        rows = jnp.concatenate(
            [block[:, :, :8].reshape(count * xs * 8, NZ), block[:, :, 8:].reshape(count * xs * 8, NZ)], axis=1)
        high, low = split(rows)
        prod = dot(high, tz[...])
        z = (prod[:, :128] + prod[:, 128:] + dot(low, tz[:, :128])).reshape(count, xs, 8, 128)
        return [[lanes16([z[g * 16 + c, q] for c in range(16)], lane) for g in range(count // 16)] for q in range(xs)]

    def z_both(xq, c):
        for q, (tiles,) in enumerate(z_tiles(32, 16, xq * 4, 4)):
            for g in range(G):
                send1[TB, g, pl.ds(xq * 32 + q * 8, 8), :] = tiles[g]
        return c

    def z_pair(xq, c):
        for q, (even, odd) in enumerate(z_tiles(0, 32, xq * 2, 2)):
            for g in range(G):
                a, b = trade(even[g], odd[g], 16, lane)
                send1[TA, g, pl.ds(xq * 16 + q * 8, 8), :] = a
                send1[TC, g, pl.ds(xq * 16 + q * 8, 8), :] = b
        return c

    first_table.wait()
    field_part(0).wait()
    z_both(0, 0)
    pl.semaphore_wait(barrier, G + H - 2)
    send1_all(TB, 0, 32)
    for copy in conv_copies:
        copy.start()
    field_part(1).wait()
    z_both(1, 0)
    send1_all(TB, 32, 32)
    field_copy(0).wait()
    field_copy(1).wait()
    for half in range(2):
        lax.fori_loop(half * 2, half * 2 + 2, z_pair, 0)
    send1_all(TA, 0, 64)
    send1_all(TC, 0, 64)
    for t in range(CT):
        recv1[t, pl.ds(me * 64, 64), :] = send1[t, me]

    for copy in const_copies:
        copy.start()
    for r in range(2):
        for q in range(2):
            weight_copy(r, q).start()

    for copy in conv_copies:
        copy.wait()
    row = lax.broadcasted_iota(jnp.int32, (384, CH), 0)
    col = lax.broadcasted_iota(jnp.int32, (384, CH), 1)
    pick = row // 8 == col
    shift[...] = jnp.sum(jnp.where(pick, bias[...], 0.0), axis=1, keepdims=True) + jnp.zeros((384, 128), F32)
    picked = pick.astype(F32).astype(BF)
    row = lax.broadcasted_iota(jnp.int32, (384, 384), 0)
    col = lax.broadcasted_iota(jnp.int32, (384, 384), 1)
    same = (row % 8) == (col % 8)
    for piece, ref in zip(split(point[...]), (a_high, a_low)):
        tall = lax.dot_general(picked, piece, (((1,), (1,)), ((), ())), preferred_element_type=F32)
        full = lax.dot_general(tall.astype(BF), picked, (((1,), (1,)), ((), ())), preferred_element_type=F32)
        ref[...] = jnp.where(same, full, 0.0).astype(BF)

    def local_step(x, c):
        for h in range(2):
            high, low = split(f_in[:, x, h * 8:(h + 1) * 8, :].reshape(384, NZ))
            local = dot(a_high[...], high) + dot(a_low[...], high) + dot(a_high[...], low) + shift[:, :1]
            held[:, x, h * 8:(h + 1) * 8, :] = local.reshape(CH, 8, NZ)
        return c

    lax.fori_loop(0, 8, local_step, 0)

    def along_x(t):
        for pair in range(4):
            data = jnp.concatenate(
                [recv1[t, pl.ds(2 * pair + h, 128, stride=8), :] for h in range(2)], axis=1)
            prod = dot(lx[...], jnp.concatenate(split(data), axis=0))
            prod = prod[:64] + prod[64:]
            for h in range(2):
                piece = prod[:, h * 128:(h + 1) * 128]
                send2[t, pl.ds(2 * pair + h, 32, stride=8), :] = piece[:32] + sign * pltpu.roll(piece[32:], 64, 1)
        send_all(copy2, t, my, H)
        recv2[t, pl.ds(my * 32, 32), :] = send2[t, pl.ds(my * 32, 32), :]

    def along_y(t):
        all2(t).wait_recv()
        data = recv2[t].reshape(H, 4, 8, 128)
        data = jnp.concatenate([data[:, i].reshape(64, 128) for i in range(4)], axis=1)
        prod = dot(ly[...], jnp.concatenate(split(data), axis=0))
        prod = prod[:128] + prod[128:]
        rows = []
        for i in range(4):
            piece = prod[:, i * 128:(i + 1) * 128]
            u = jnp.where(first, piece[:32], piece[64:96])
            w = jnp.where(first, piece[32:64], piece[96:])
            v = u + sign * pltpu.roll(w, 64, 1)
            rows.append(v + pltpu.roll(v, 32, 1))
        v = jnp.concatenate(rows, axis=0)
        v_exp[t] = dot(jnp.concatenate(split(v), axis=1), e_in[1 if t == TB else 0])

    def mix(q):
        t = (TA, TC)[q]

        def body(i, c):
            at = pl.ds(pl.multiple_of(i * 32, 32), 32)
            for part in range(3):
                real = jnp.zeros((32, 128), F32)
                imag = jnp.zeros((32, 128), F32)
                for b in range(6):
                    col = b * 384 + part * 128
                    if b < 4:
                        source, base, gap = t, b * 768 + part * 128, 384
                    else:
                        source, base, gap = TB, (b - 4) * 1536 + q * 384 + part * 128, 768
                    vr = v_exp[source, at, base:base + 128]
                    vi = v_exp[source, at, base + gap:base + gap + 128]
                    w0 = w_in[0, q, i, :, col:col + 128]
                    w1 = w_in[1, q, i, :, col:col + 128]
                    real += vr * w0 - vi * w1
                    imag += vr * w1 + vi * w0
                col = q * 768 + part * 128
                h_acc[at, col:col + 128] = real
                h_acc[at, col + 384:col + 384 + 128] = imag
            return c

        lax.fori_loop(0, 4, body, 0)

    def collect(t):
        if t == TB:
            source, table = h_acc[...], r_in[768:, :]
        else:
            source, table = h_acc[:, (0 if t == TA else 768):(768 if t == TA else 1536)], r_in[:768, :]
        both = dot(jnp.concatenate(split(source), axis=0), table)
        return both[:128] + both[128:]

    def back_y(t):
        h_all = collect(t)
        data = jnp.concatenate([h_all[i * 32:(i + 1) * 32] for i in range(4)], axis=1)
        high, low = split(data)
        prod = dot(liy[...], jnp.concatenate([high, low, high], axis=0))
        for i in range(4):
            piece = prod[:, i * 128:(i + 1) * 128]
            a = jnp.where(first, piece[:64], piece[64:128])
            b = jnp.where(first, piece[128:192], piece[192:])
            q = a - sign * pltpu.roll(b, 64, 1)
            send3[t, :, i * 8:(i + 1) * 8, :] = q.reshape(H, 8, 128)
        send_all(copy3, t, my, H)
        recv3[t, pl.ds(my * 32, 32), :] = send3[t, my]

    def back_x(t):
        all3(t).wait_recv()
        for pair in range(4):
            data = jnp.concatenate(
                [recv3[t, pl.ds(2 * pair + h, 32, stride=8), :] for h in range(2)], axis=1)
            high, low = split(data)
            prod = dot(lix[...], jnp.concatenate([high, low, high], axis=0))
            for h in range(2):
                piece = prod[:, h * 128:(h + 1) * 128]
                send4[t, pl.ds(2 * pair + h, 128, stride=8), :] = piece[:128] - sign * pltpu.roll(piece[128:], 64, 1)
        send_all(copy4, t, me, G)
        if t == TB:
            own4().start()
        else:
            recv4[t, me] = send4[t, pl.ds(me * 64, 64), :]

    for copy in const_copies:
        copy.wait()
    all1(TB).wait_recv()
    along_x(TB)
    all1(TA).wait_recv()
    along_x(TA)
    for r in range(2):
        for q in range(2):
            weight_copy(r, q).wait()
    along_y(TB)
    all1(TC).wait_recv()
    along_x(TC)
    along_y(TA)
    mix(0)
    back_y(TA)
    along_y(TC)
    mix(1)
    back_y(TC)
    back_x(TA)
    back_y(TB)
    back_x(TC)
    back_x(TB)

    for t in range(CT):
        all1(t).wait_send()
        all2(t).wait_send()
        all3(t).wait_send()
    all4(TA).wait_recv()

    def turn(x, c):
        at = pl.ds(pl.multiple_of(x * 8, 8), 8)
        for o, tile in enumerate(lanes16([recv4[TA, s, at, :] for s in range(G)], lane)):
            recv4[TA, o, at, :] = tile
        return c

    lax.fori_loop(0, 8, turn, 0)
    all4(TC).wait_recv()

    def finish(xq, c):
        tiles = []
        for x in range(2):
            at = pl.ds(xq * 16 + x * 8, 8)
            odd = lanes16([recv4[TC, s, at, :] for s in range(G)], lane)
            tiles.append([trade(recv4[TA, o, at, :], odd[o], 16, lane) for o in range(16)])
        rows = jnp.concatenate([tiles[x][o][p] for p in range(2) for o in range(16) for x in range(2)], axis=0)
        high, low = split(rows)
        spectral = dot(jnp.concatenate([high, low], axis=1), ez_in[...]) + dot(high, el_in[...])
        for h in range(2):
            at = (pl.ds(0, 32), pl.ds(xq * 2, 2), pl.ds(h * 8, 8), slice(None))
            held[at] = gelu(held[at] + spectral[:, h * NZ:(h + 1) * NZ].reshape(32, 2, 8, NZ))
        return c

    lax.fori_loop(0, 4, finish, 0)
    for t in range(CT):
        all4(t).wait_send()
    own4().wait()
    all4(TB).wait_recv()


def final_kernel(pre, modes, ez, el, out, work, ez_in, el_in, v_sem, o_sem, c_sem):
    lane = lax.broadcasted_iota(jnp.int32, (8, 128), 1)
    done = CH - 16
    small = [pltpu.make_async_copy(ez, ez_in, c_sem.at[0]), pltpu.make_async_copy(el, el_in, c_sem.at[1])]
    store = [pltpu.make_async_copy(work.at[p], out.at[pl.ds(done, 16), pl.ds(2 * p, 2)], v_sem.at[p]) for p in range(4)]
    give = [pltpu.make_async_copy(pre.at[pl.ds(8 * p, 8)], out.at[pl.ds(8 * p, 8)], o_sem.at[p]) for p in range(4)]
    for copy in small + give:
        copy.start()
    for p in range(4):
        tiles = [lanes16([modes[s, p * 16 + x * 8:p * 16 + (x + 1) * 8, :] for s in range(G)], lane) for x in range(2)]
        high, low = split(jnp.concatenate([tile[o] for o in range(16) for tile in tiles], axis=0))
        if p == 0:
            for copy in small:
                copy.wait()
        spectral = dot(jnp.concatenate([high, low], axis=1), ez_in[...]) + dot(high, el_in[...])
        for h in range(2):
            y = slice(h * 8, (h + 1) * 8)
            part = spectral[:, h * NZ:(h + 1) * NZ].reshape(16, 2, 8, NZ)
            work[p, :, :, y, :] = gelu(pre[done:, 2 * p:2 * p + 2, y, :] + part)
        store[p].start()
    for copy in store + give:
        copy.wait()


def far(array):
    return pltpu.with_memory_space_constraint(array, pltpu.HBM)


def shards(field, spectral_weight, pointwise_weight, channel_bias):
    tz, lx, ly, spread, gather, liy, lix, ez, el = [far(jnp.asarray(c)) for c in constants()]
    field = field.reshape(field.shape[1:])
    scratch = [
        pltpu.VMEM((CH, 8, 16, NZ), F32),
        pltpu.VMEM((2, 2, 4, MODES, CH * CH), F32),
        pltpu.VMEM(spread.shape, BF),
        pltpu.VMEM(gather.shape, BF),
        pltpu.VMEM(ez.shape, BF),
        pltpu.VMEM(el.shape, BF),
        pltpu.VMEM(tz.shape, BF),
        pltpu.VMEM(lx.shape, BF),
        pltpu.VMEM(ly.shape, BF),
        pltpu.VMEM(liy.shape, BF),
        pltpu.VMEM(lix.shape, BF),
        pltpu.VMEM((CH, CH), F32),
        pltpu.VMEM((1, CH), F32),
        pltpu.VMEM((384, 384), BF),
        pltpu.VMEM((384, 384), BF),
        pltpu.VMEM((384, 128), F32),
        pltpu.VMEM((CT, G, 64, 128), F32),
        pltpu.VMEM((CT, G * 64 + 8, 128), F32),
        pltpu.VMEM((CT, H * 32 + 8, 128), F32),
        pltpu.VMEM((CT, H * 32, 128), F32),
        pltpu.VMEM((CT, H, 32, 128), F32),
        pltpu.VMEM((CT, H * 32 + 8, 128), F32),
        pltpu.VMEM((CT, G * 64 + 8, 128), F32),
        pltpu.VMEM((2, G, 64, 128), F32),
        pltpu.VMEM((CT, 128, 3072), F32),
        pltpu.VMEM((128, 1536), F32),
    ]
    dma = pltpu.SemaphoreType.DMA
    scratch += [dma((4,)), dma((2, 2)), dma((11,))]
    scratch += [dma((CT,))] * 8 + [dma]
    pre, last = pl.pallas_call(
        spectral_kernel,
        out_shape=[pltpu.VMEM(field.shape, F32), pltpu.VMEM((G, 64, 128), F32)],
        in_specs=[ANY] * 13,
        out_specs=[VMEM] * 2,
        scratch_shapes=scratch,
        compiler_params=pltpu.CompilerParams(
            collective_id=0, has_side_effects=True, vmem_limit_bytes=46 * 1024 * 1024),
        name="spectral",
    )(far(field), far(spectral_weight), spread, gather, ez, el, far(pointwise_weight), far(channel_bias.reshape(1, CH)),
      tz, lx, ly, liy, lix)
    out = pl.pallas_call(
        final_kernel,
        out_shape=jax.ShapeDtypeStruct(field.shape, F32),
        in_specs=[VMEM, VMEM, ANY, ANY],
        out_specs=ANY,
        scratch_shapes=[
            pltpu.VMEM((4, 16, 2, 16, NZ), F32),
            pltpu.VMEM(ez.shape, BF),
            pltpu.VMEM(el.shape, BF),
            dma((4,)), dma((4,)), dma((2,)),
        ],
        compiler_params=pltpu.CompilerParams(vmem_limit_bytes=40 * 1024 * 1024),
        name="physical",
    )(pre, last, ez, el)
    return out.reshape((1,) + out.shape)


def solution(mesh):
    in_specs = (P(None, None, "px", "py", None), P(None, "py", None, "px", None), P(), P())
    out_specs = P(None, None, "px", "py", None)
    return jax.shard_map(shards, mesh=mesh, in_specs=in_specs, out_specs=out_specs, check_vma=False)
```

```python
import functools
import math

import jax
import jax.numpy as jnp
import ml_dtypes
import numpy as np
from jax import lax
from jax.experimental import pallas as pl
from jax.experimental.pallas import tpu as pltpu
from jax.sharding import PartitionSpec as P

MESH = pl.DeviceIdType.MESH
BF = jnp.bfloat16
F32 = jnp.float32
ANY = pl.BlockSpec(memory_space=pl.ANY)
VMEM = pl.BlockSpec(memory_space=pltpu.VMEM)

NX, NY, NZ, MODES, CH, G, H = 128, 128, 256, 32, 48, 16, 8
CT = CH // 16
TA, TC, TB = range(3)


def halves(table):
    high = table.astype(ml_dtypes.bfloat16)
    low = (table - high.astype(np.float64)).astype(ml_dtypes.bfloat16)
    return high, low


def signed(modes):
    number = np.arange(modes)
    return np.where(number < modes // 2, number, number - modes)


def angles(position, mode, length):
    return 2.0 * math.pi * ((position[:, None] * mode[None, :]) % length) / length


def lane_parts():
    lane = np.arange(128)
    return lane // 64, (lane // 32) % 2, (lane // 16) % 2, lane % 16


@functools.cache
def constants():
    ri, y2, k2, low = lane_parts()
    k = 2 * low + k2
    a = angles(np.arange(NZ), k, NZ)
    wave = np.where(ri[None, :] == 0, np.cos(a), -np.sin(a))
    forward = np.concatenate([wave * (y2 == 0), wave * (y2 == 1)], axis=0)
    tz = np.concatenate(halves(forward), axis=1)
    gain = np.where(k == 0, 1.0, 2.0) / (NX * NY * NZ)
    eh, el = halves((forward * gain).T)
    ez = np.concatenate([eh, eh], axis=0)
    f = signed(MODES)
    ax = angles(np.arange(NX), f, NX)
    ch, cl = halves(np.concatenate([np.cos(ax).T, np.sin(ax).T], axis=0))
    lx = np.concatenate(
        [np.concatenate([ch, ch], axis=1), np.concatenate([cl, np.zeros_like(cl)], axis=1)], axis=0
    )
    ch, cl = halves(np.concatenate([np.cos(ax), np.sin(ax)], axis=0))
    lix = np.concatenate([ch, ch, cl], axis=1)
    y = np.arange(NY).reshape(H, 2, 8)
    parts = [y[:, h].reshape(-1) for h in range(2)]
    ay = [angles(p, f, NY) for p in parts]
    rows = np.concatenate([t for q in ay for t in (np.cos(q).T, np.sin(q).T)], axis=0)
    ch, cl = halves(rows)
    ly = np.concatenate(
        [np.concatenate([ch, ch], axis=1), np.concatenate([cl, np.zeros_like(cl)], axis=1)], axis=0
    )
    rows = np.concatenate([np.cos(ay[0]), np.cos(ay[1]), np.sin(ay[0]), np.sin(ay[1])], axis=0)
    ch, cl = halves(rows)
    liy = np.concatenate([ch, ch, cl], axis=1)
    pair = np.zeros((128, 4, 2, 8, CH))
    both = np.zeros((128, 2, 2, 2, 8, CH))
    for r in range(2):
        for c in range(32):
            pair[r * 64 + 32 + c, c // 8, r, c % 8, :] = 1.0
        for q in range(2):
            for c in range(16):
                both[r * 64 + 32 + q * 16 + c, c // 8, r, q, c % 8, :] = 1.0
    spread = np.stack([pair.reshape(128, -1), both.reshape(128, -1)])
    spread = np.concatenate([spread, spread], axis=1).astype(ml_dtypes.bfloat16)
    pair = np.zeros((2, 8, CH, 128))
    both = np.zeros((2, 2, 8, CH, 128))
    for r in range(2):
        for h in range(2):
            for o in range(32):
                pair[r, :, o, r * 64 + h * 32 + o] = 1.0
            for q in range(2):
                for o in range(16):
                    both[q, r, :, 32 + o, r * 64 + h * 32 + q * 16 + o] = 1.0
    gather = np.concatenate([pair.reshape(-1, 128), both.reshape(-1, 128)], axis=0).astype(ml_dtypes.bfloat16)
    return tz, lx, ly, spread, gather, liy, lix, ez, el


def split(value):
    high = value.astype(BF)
    return high, (value - high.astype(F32)).astype(BF)


def dot(a, b):
    return jnp.dot(a, b, preferred_element_type=F32)


def trade(a, b, step, lane):
    keep = (lane & step) == 0
    return jnp.where(keep, a, pltpu.roll(b, step, 1)), jnp.where(keep, pltpu.roll(a, 128 - step, 1), b)


def lanes16(tiles, lane):
    tiles = [pltpu.roll(tile, c, 1) if c else tile for c, tile in enumerate(tiles)]
    for bit in range(4):
        step = 1 << bit
        shift = (lane & step) != 0
        tiles = [jnp.where(shift, tiles[(h + step) % 16], tiles[h]) for h in range(16)]
    return [pltpu.roll(tiles[16 - g], 128 - g, 1) if g else tiles[0] for g in range(16)]


def gelu(v):
    return 0.5 * v * (1.0 + lax.erf(v * math.sqrt(0.5)))


def spectral_kernel(
    field, weight, spread, gather, ez, el, point_far, bias_far, tz_far, lx_far, ly_far, liy_far, lix_far, held, last,
    f_in, w_in, e_in, r_in, ez_in, el_in, tz, lx, ly, liy, lix, point, bias, a_high, a_low, shift,
    send1, recv1, send2, recv2, send3, recv3, send4, recv4, v_exp, h_acc,
    f_sem, w_sem, c_sem, s1, r1, s2, r2, s3, r3, s4, r4, o_sem,
):
    me, my = lax.axis_index("px"), lax.axis_index("py")

    def field_copy(t):
        return pltpu.make_async_copy(field.at[pl.ds(t * 16, 16)], f_in.at[pl.ds(t * 16, 16)], f_sem.at[t])

    def field_part(half):
        at = (pl.ds(32, 16), pl.ds(half * 4, 4))
        return pltpu.make_async_copy(field.at[at], f_in.at[at], f_sem.at[2 + half])

    def weight_copy(r, q):
        return pltpu.make_async_copy(weight.at[r, :, :, q, :], w_in.at[r, q], w_sem.at[r, q])

    const_copies = [
        pltpu.make_async_copy(spread, e_in, c_sem.at[0]),
        pltpu.make_async_copy(gather, r_in, c_sem.at[1]),
        pltpu.make_async_copy(ez, ez_in, c_sem.at[2]),
        pltpu.make_async_copy(el, el_in, c_sem.at[3]),
        pltpu.make_async_copy(lx_far, lx, c_sem.at[4]),
        pltpu.make_async_copy(ly_far, ly, c_sem.at[5]),
        pltpu.make_async_copy(liy_far, liy, c_sem.at[6]),
        pltpu.make_async_copy(lix_far, lix, c_sem.at[7]),
    ]
    conv_copies = [
        pltpu.make_async_copy(point_far, point, c_sem.at[9]),
        pltpu.make_async_copy(bias_far, bias, c_sem.at[10]),
    ]
    first_table = pltpu.make_async_copy(tz_far, tz, c_sem.at[8])
    first_table.start()
    for half in range(2):
        field_part(half).start()
    for t in range(2):
        field_copy(t).start()

    barrier = pltpu.get_barrier_semaphore()

    def greet_x(d, c):
        pl.semaphore_signal(barrier, inc=1, device_id=(lax.rem(me + d, G), my), device_id_type=MESH)
        return c

    def greet_y(d, c):
        pl.semaphore_signal(barrier, inc=1, device_id=(me, lax.rem(my + d, H)), device_id_type=MESH)
        return c

    lax.fori_loop(1, G, greet_x, 0)
    lax.fori_loop(1, H, greet_y, 0)

    def copy1(t, first_row, rows, target, source):
        return pltpu.make_async_remote_copy(
            send1.at[t, target, pl.ds(first_row, rows)], recv1.at[t, pl.ds(source * 64 + first_row, rows)],
            s1.at[t], r1.at[t], device_id=(target, my), device_id_type=MESH)

    def send1_all(t, first_row, rows):
        def body(d, c):
            copy1(t, first_row, rows, lax.rem(me + d, G), me).start()
            return c
        lax.fori_loop(1, G, body, 0)

    def copy2(t, target, source):
        return pltpu.make_async_remote_copy(
            send2.at[t, pl.ds(target * 32, 32)], recv2.at[t, pl.ds(source * 32, 32)], s2.at[t],
            r2.at[t], device_id=(me, target), device_id_type=MESH)

    def copy3(t, target, source):
        return pltpu.make_async_remote_copy(
            send3.at[t, target], recv3.at[t, pl.ds(source * 32, 32)], s3.at[t], r3.at[t],
            device_id=(me, target), device_id_type=MESH)

    def landing(t):
        return last if t == TB else recv4.at[t]

    def copy4(t, target, source):
        return pltpu.make_async_remote_copy(
            send4.at[t, pl.ds(target * 64, 64)], landing(t).at[source], s4.at[t], r4.at[t],
            device_id=(target, my), device_id_type=MESH)

    def own4():
        return pltpu.make_async_copy(send4.at[TB, pl.ds(me * 64, 64)], last.at[me], o_sem)

    def send_all(copy, t, index, count):
        def body(d, c):
            copy(t, lax.rem(index + d, count), index).start()
            return c
        lax.fori_loop(1, count, body, 0)

    def all1(t):
        return pltpu.make_async_remote_copy(
            send1.at[t, pl.ds(0, G - 1)], recv1.at[t, pl.ds(0, (G - 1) * 64)], s1.at[t], r1.at[t],
            device_id=(lax.rem(me + 1, G), my), device_id_type=MESH)

    def all2(t):
        return pltpu.make_async_remote_copy(
            send2.at[t, pl.ds(0, (H - 1) * 32)], recv2.at[t, pl.ds(0, (H - 1) * 32)], s2.at[t], r2.at[t],
            device_id=(me, lax.rem(my + 1, H)), device_id_type=MESH)

    def all3(t):
        return pltpu.make_async_remote_copy(
            send3.at[t, pl.ds(0, H - 1)], recv3.at[t, pl.ds(0, (H - 1) * 32)], s3.at[t], r3.at[t],
            device_id=(me, lax.rem(my + 1, H)), device_id_type=MESH)

    def all4(t):
        return pltpu.make_async_remote_copy(
            send4.at[t, pl.ds(0, (G - 1) * 64)], landing(t).at[pl.ds(0, G - 1)], s4.at[t], r4.at[t],
            device_id=(lax.rem(me + 1, G), my), device_id_type=MESH)

    lane = lax.broadcasted_iota(jnp.int32, (8, 128), 1)
    wide = lax.broadcasted_iota(jnp.int32, (1, 128), 1)
    sign = jnp.where(wide < 64, 1.0, -1.0).astype(F32)
    first = (wide & 32) == 0

    def z_tiles(first_c, count, x, xs):
        block = f_in[first_c:first_c + count, pl.ds(x, xs)]
        rows = jnp.concatenate(
            [block[:, :, :8].reshape(count * xs * 8, NZ), block[:, :, 8:].reshape(count * xs * 8, NZ)], axis=1)
        high, low = split(rows)
        prod = dot(high, tz[...])
        z = (prod[:, :128] + prod[:, 128:] + dot(low, tz[:, :128])).reshape(count, xs, 8, 128)
        return [[lanes16([z[g * 16 + c, q] for c in range(16)], lane) for g in range(count // 16)] for q in range(xs)]

    def z_both(xq, c):
        for q, (tiles,) in enumerate(z_tiles(32, 16, xq * 4, 4)):
            for g in range(G):
                send1[TB, g, pl.ds(xq * 32 + q * 8, 8), :] = tiles[g]
        return c

    def z_pair(xq, c):
        for q, (even, odd) in enumerate(z_tiles(0, 32, xq * 2, 2)):
            for g in range(G):
                a, b = trade(even[g], odd[g], 16, lane)
                send1[TA, g, pl.ds(xq * 16 + q * 8, 8), :] = a
                send1[TC, g, pl.ds(xq * 16 + q * 8, 8), :] = b
        return c

    first_table.wait()
    field_part(0).wait()
    z_both(0, 0)
    pl.semaphore_wait(barrier, G + H - 2)
    send1_all(TB, 0, 32)
    for copy in conv_copies:
        copy.start()
    field_part(1).wait()
    z_both(1, 0)
    send1_all(TB, 32, 32)
    field_copy(0).wait()
    field_copy(1).wait()
    for half in range(2):
        lax.fori_loop(half * 2, half * 2 + 2, z_pair, 0)
    send1_all(TA, 0, 64)
    send1_all(TC, 0, 64)
    for t in range(CT):
        recv1[t, pl.ds(me * 64, 64), :] = send1[t, me]

    for copy in const_copies:
        copy.start()
    for r in range(2):
        for q in range(2):
            weight_copy(r, q).start()

    for copy in conv_copies:
        copy.wait()
    row = lax.broadcasted_iota(jnp.int32, (384, CH), 0)
    col = lax.broadcasted_iota(jnp.int32, (384, CH), 1)
    pick = row // 8 == col
    shift[...] = jnp.sum(jnp.where(pick, bias[...], 0.0), axis=1, keepdims=True) + jnp.zeros((384, 128), F32)
    picked = pick.astype(F32).astype(BF)
    row = lax.broadcasted_iota(jnp.int32, (384, 384), 0)
    col = lax.broadcasted_iota(jnp.int32, (384, 384), 1)
    same = (row % 8) == (col % 8)
    for piece, ref in zip(split(point[...]), (a_high, a_low)):
        tall = lax.dot_general(picked, piece, (((1,), (1,)), ((), ())), preferred_element_type=F32)
        full = lax.dot_general(tall.astype(BF), picked, (((1,), (1,)), ((), ())), preferred_element_type=F32)
        ref[...] = jnp.where(same, full, 0.0).astype(BF)

    def local_step(x, c):
        for h in range(2):
            high, low = split(f_in[:, x, h * 8:(h + 1) * 8, :].reshape(384, NZ))
            local = dot(a_high[...], high) + dot(a_low[...], high) + dot(a_high[...], low) + shift[:, :1]
            held[:, x, h * 8:(h + 1) * 8, :] = local.reshape(CH, 8, NZ)
        return c

    lax.fori_loop(0, 8, local_step, 0)

    def along_x(t):
        for pair in range(4):
            data = jnp.concatenate(
                [recv1[t, pl.ds(2 * pair + h, 128, stride=8), :] for h in range(2)], axis=1)
            prod = dot(lx[...], jnp.concatenate(split(data), axis=0))
            prod = prod[:64] + prod[64:]
            for h in range(2):
                piece = prod[:, h * 128:(h + 1) * 128]
                send2[t, pl.ds(2 * pair + h, 32, stride=8), :] = piece[:32] + sign * pltpu.roll(piece[32:], 64, 1)
        send_all(copy2, t, my, H)
        recv2[t, pl.ds(my * 32, 32), :] = send2[t, pl.ds(my * 32, 32), :]

    def along_y(t):
        all2(t).wait_recv()
        data = recv2[t].reshape(H, 4, 8, 128)
        data = jnp.concatenate([data[:, i].reshape(64, 128) for i in range(4)], axis=1)
        prod = dot(ly[...], jnp.concatenate(split(data), axis=0))
        prod = prod[:128] + prod[128:]
        rows = []
        for i in range(4):
            piece = prod[:, i * 128:(i + 1) * 128]
            u = jnp.where(first, piece[:32], piece[64:96])
            w = jnp.where(first, piece[32:64], piece[96:])
            v = u + sign * pltpu.roll(w, 64, 1)
            rows.append(v + pltpu.roll(v, 32, 1))
        v = jnp.concatenate(rows, axis=0)
        v_exp[t] = dot(jnp.concatenate(split(v), axis=1), e_in[1 if t == TB else 0])

    def mix(q):
        t = (TA, TC)[q]

        def body(i, c):
            at = pl.ds(pl.multiple_of(i * 32, 32), 32)
            for part in range(3):
                real = jnp.zeros((32, 128), F32)
                imag = jnp.zeros((32, 128), F32)
                for b in range(6):
                    col = b * 384 + part * 128
                    if b < 4:
                        source, base, gap = t, b * 768 + part * 128, 384
                    else:
                        source, base, gap = TB, (b - 4) * 1536 + q * 384 + part * 128, 768
                    vr = v_exp[source, at, base:base + 128]
                    vi = v_exp[source, at, base + gap:base + gap + 128]
                    w0 = w_in[0, q, i, :, col:col + 128]
                    w1 = w_in[1, q, i, :, col:col + 128]
                    real += vr * w0 - vi * w1
                    imag += vr * w1 + vi * w0
                col = q * 768 + part * 128
                h_acc[at, col:col + 128] = real
                h_acc[at, col + 384:col + 384 + 128] = imag
            return c

        lax.fori_loop(0, 4, body, 0)

    def collect(t):
        if t == TB:
            source, table = h_acc[...], r_in[768:, :]
        else:
            source, table = h_acc[:, (0 if t == TA else 768):(768 if t == TA else 1536)], r_in[:768, :]
        both = dot(jnp.concatenate(split(source), axis=0), table)
        return both[:128] + both[128:]

    def back_y(t):
        h_all = collect(t)
        data = jnp.concatenate([h_all[i * 32:(i + 1) * 32] for i in range(4)], axis=1)
        high, low = split(data)
        prod = dot(liy[...], jnp.concatenate([high, low, high], axis=0))
        for i in range(4):
            piece = prod[:, i * 128:(i + 1) * 128]
            a = jnp.where(first, piece[:64], piece[64:128])
            b = jnp.where(first, piece[128:192], piece[192:])
            q = a - sign * pltpu.roll(b, 64, 1)
            send3[t, :, i * 8:(i + 1) * 8, :] = q.reshape(H, 8, 128)
        send_all(copy3, t, my, H)
        recv3[t, pl.ds(my * 32, 32), :] = send3[t, my]

    def back_x(t):
        all3(t).wait_recv()
        for pair in range(4):
            data = jnp.concatenate(
                [recv3[t, pl.ds(2 * pair + h, 32, stride=8), :] for h in range(2)], axis=1)
            high, low = split(data)
            prod = dot(lix[...], jnp.concatenate([high, low, high], axis=0))
            for h in range(2):
                piece = prod[:, h * 128:(h + 1) * 128]
                send4[t, pl.ds(2 * pair + h, 128, stride=8), :] = piece[:128] - sign * pltpu.roll(piece[128:], 64, 1)
        send_all(copy4, t, me, G)
        if t == TB:
            own4().start()
        else:
            recv4[t, me] = send4[t, pl.ds(me * 64, 64), :]

    for copy in const_copies:
        copy.wait()
    all1(TB).wait_recv()
    along_x(TB)
    all1(TA).wait_recv()
    along_x(TA)
    for r in range(2):
        for q in range(2):
            weight_copy(r, q).wait()
    along_y(TB)
    all1(TC).wait_recv()
    along_x(TC)
    along_y(TA)
    mix(0)
    back_y(TA)
    along_y(TC)
    mix(1)
    back_y(TC)
    back_x(TA)
    back_y(TB)
    back_x(TC)
    back_x(TB)

    for t in range(CT):
        all1(t).wait_send()
        all2(t).wait_send()
        all3(t).wait_send()
    all4(TA).wait_recv()

    def turn(x, c):
        at = pl.ds(pl.multiple_of(x * 8, 8), 8)
        for o, tile in enumerate(lanes16([recv4[TA, s, at, :] for s in range(G)], lane)):
            recv4[TA, o, at, :] = tile
        return c

    lax.fori_loop(0, 8, turn, 0)
    all4(TC).wait_recv()

    def finish(xq, c):
        tiles = []
        for x in range(2):
            at = pl.ds(xq * 16 + x * 8, 8)
            odd = lanes16([recv4[TC, s, at, :] for s in range(G)], lane)
            tiles.append([trade(recv4[TA, o, at, :], odd[o], 16, lane) for o in range(16)])
        rows = jnp.concatenate([tiles[x][o][p] for p in range(2) for o in range(16) for x in range(2)], axis=0)
        high, low = split(rows)
        spectral = dot(jnp.concatenate([high, low], axis=1), ez_in[...]) + dot(high, el_in[...])
        for h in range(2):
            at = (pl.ds(0, 32), pl.ds(xq * 2, 2), pl.ds(h * 8, 8), slice(None))
            held[at] = gelu(held[at] + spectral[:, h * NZ:(h + 1) * NZ].reshape(32, 2, 8, NZ))
        return c

    lax.fori_loop(0, 4, finish, 0)
    for t in range(CT):
        all4(t).wait_send()
    own4().wait()
    all4(TB).wait_recv()


def final_kernel(pre, modes, ez, el, out, work, ez_in, el_in, v_sem, o_sem, c_sem):
    lane = lax.broadcasted_iota(jnp.int32, (8, 128), 1)
    done = CH - 16
    small = [pltpu.make_async_copy(ez, ez_in, c_sem.at[0]), pltpu.make_async_copy(el, el_in, c_sem.at[1])]
    store = [pltpu.make_async_copy(work.at[p], out.at[pl.ds(done, 16), pl.ds(4 * p, 4)], v_sem.at[p]) for p in range(2)]
    give = [pltpu.make_async_copy(pre.at[pl.ds(8 * p, 8)], out.at[pl.ds(8 * p, 8)], o_sem.at[p]) for p in range(4)]
    for copy in small + give:
        copy.start()
    for p in range(2):
        tiles = [lanes16([modes[s, p * 32 + x * 8:p * 32 + (x + 1) * 8, :] for s in range(G)], lane) for x in range(4)]
        high, low = split(jnp.concatenate([tile[o] for o in range(16) for tile in tiles], axis=0))
        if p == 0:
            for copy in small:
                copy.wait()
        spectral = dot(jnp.concatenate([high, low], axis=1), ez_in[...]) + dot(high, el_in[...])
        for h in range(2):
            y = slice(h * 8, (h + 1) * 8)
            part = spectral[:, h * NZ:(h + 1) * NZ].reshape(16, 4, 8, NZ)
            work[p, :, :, y, :] = gelu(pre[done:, 4 * p:4 * p + 4, y, :] + part)
        store[p].start()
    for copy in store + give:
        copy.wait()


def far(array):
    return pltpu.with_memory_space_constraint(array, pltpu.HBM)


def shards(field, spectral_weight, pointwise_weight, channel_bias):
    tz, lx, ly, spread, gather, liy, lix, ez, el = [far(jnp.asarray(c)) for c in constants()]
    field = field.reshape(field.shape[1:])
    scratch = [
        pltpu.VMEM((CH, 8, 16, NZ), F32),
        pltpu.VMEM((2, 2, 4, MODES, CH * CH), F32),
        pltpu.VMEM(spread.shape, BF),
        pltpu.VMEM(gather.shape, BF),
        pltpu.VMEM(ez.shape, BF),
        pltpu.VMEM(el.shape, BF),
        pltpu.VMEM(tz.shape, BF),
        pltpu.VMEM(lx.shape, BF),
        pltpu.VMEM(ly.shape, BF),
        pltpu.VMEM(liy.shape, BF),
        pltpu.VMEM(lix.shape, BF),
        pltpu.VMEM((CH, CH), F32),
        pltpu.VMEM((1, CH), F32),
        pltpu.VMEM((384, 384), BF),
        pltpu.VMEM((384, 384), BF),
        pltpu.VMEM((384, 128), F32),
        pltpu.VMEM((CT, G, 64, 128), F32),
        pltpu.VMEM((CT, G * 64 + 8, 128), F32),
        pltpu.VMEM((CT, H * 32 + 8, 128), F32),
        pltpu.VMEM((CT, H * 32, 128), F32),
        pltpu.VMEM((CT, H, 32, 128), F32),
        pltpu.VMEM((CT, H * 32 + 8, 128), F32),
        pltpu.VMEM((CT, G * 64 + 8, 128), F32),
        pltpu.VMEM((2, G, 64, 128), F32),
        pltpu.VMEM((CT, 128, 3072), F32),
        pltpu.VMEM((128, 1536), F32),
    ]
    dma = pltpu.SemaphoreType.DMA
    scratch += [dma((4,)), dma((2, 2)), dma((11,))]
    scratch += [dma((CT,))] * 8 + [dma]
    pre, last = pl.pallas_call(
        spectral_kernel,
        out_shape=[pltpu.VMEM(field.shape, F32), pltpu.VMEM((G, 64, 128), F32)],
        in_specs=[ANY] * 13,
        out_specs=[VMEM] * 2,
        scratch_shapes=scratch,
        compiler_params=pltpu.CompilerParams(
            collective_id=0, has_side_effects=True, vmem_limit_bytes=46 * 1024 * 1024),
        name="spectral",
    )(far(field), far(spectral_weight), spread, gather, ez, el, far(pointwise_weight), far(channel_bias.reshape(1, CH)),
      tz, lx, ly, liy, lix)
    out = pl.pallas_call(
        final_kernel,
        out_shape=jax.ShapeDtypeStruct(field.shape, F32),
        in_specs=[VMEM, VMEM, ANY, ANY],
        out_specs=ANY,
        scratch_shapes=[
            pltpu.VMEM((2, 16, 4, 16, NZ), F32),
            pltpu.VMEM(ez.shape, BF),
            pltpu.VMEM(el.shape, BF),
            dma((4,)), dma((4,)), dma((2,)),
        ],
        compiler_params=pltpu.CompilerParams(vmem_limit_bytes=40 * 1024 * 1024),
        name="physical",
    )(pre, last, ez, el)
    return out.reshape((1,) + out.shape)


def solution(mesh):
    in_specs = (P(None, None, "px", "py", None), P(None, "py", None, "px", None), P(), P())
    out_specs = P(None, None, "px", "py", None)
    return jax.shard_map(shards, mesh=mesh, in_specs=in_specs, out_specs=out_specs, check_vma=False)
```
